32 devices in a mesh: dp: 4 (over y, x), seq: 8 (over z, core).
Axes of the slice: x: 2, y: 2, z: 4, core: 2. Of those that a mesh axis runs over, the one named last changes fastest.
Arguments:
- latents: bfloat16 [4, 3072, 1152], P('dp', 'seq'), may hold values from -9 to 9
- time_embed: bfloat16 [4, 6, 1152], P('dp'), may hold values from -3 to 3
- text_tokens: bfloat16 [4, 120, 1152], P('dp'), may hold values from -9 to 9
- cotangent: bfloat16 [4, 3072, 1152], P('dp', 'seq'), may hold values from -9 to 9
- w_attn: float32 [8, 1152, 1152], P(None, 'seq', 'dp'), may hold values from -0.70710678 to 0.70710678
- w_mlp: float32 [2, 1152, 4608], P(None, 'seq', 'dp'), may hold values from -0.176776695 to 0.176776695
- bias_table: float32 [17, 1152], P(None, 'seq'), may hold values from -0.3 to 0.3
- attn_first: float32 [8, 1152, 1152], P(None, 'seq', 'dp'), may hold values from -0.0003 to 0.0003
- attn_second: float32 [8, 1152, 1152], P(None, 'seq', 'dp'), may hold values from 2.5e-09 to 1e-08
- mlp_first: float32 [2, 1152, 4608], P(None, 'seq', 'dp'), may hold values from -0.0018 to 0.0018
- mlp_second: float32 [2, 1152, 4608], P(None, 'seq', 'dp'), may hold values from 9e-08 to 3.6e-07
- table_first: float32 [17, 1152], P(None, 'seq'), may hold values from -0.0036 to 0.0036
- table_second: float32 [17, 1152], P(None, 'seq'), may hold values from 3.6e-07 to 1.4e-06
Outputs:
- block_out: bfloat16 [4, 3072, 1152], P('dp', 'seq')
- grad_latents: float32 [4, 3072, 1152], P('dp', 'seq')
- grad_time: float32 [4, 6, 1152], P('dp')
- grad_text: float32 [4, 120, 1152], P('dp')
- grad_norm: float32 [], replicated
- attn_new: float32 [8, 1152, 1152], P(None, 'seq', 'dp')
- attn_copy: bfloat16 [8, 1152, 1152], P(None, 'seq', 'dp')
- attn_first_new: float32 [8, 1152, 1152], P(None, 'seq', 'dp')
- attn_second_new: float32 [8, 1152, 1152], P(None, 'seq', 'dp')
- mlp_new: float32 [2, 1152, 4608], P(None, 'seq', 'dp')
- mlp_copy: bfloat16 [2, 1152, 4608], P(None, 'seq', 'dp')
- mlp_first_new: float32 [2, 1152, 4608], P(None, 'seq', 'dp')
- mlp_second_new: float32 [2, 1152, 4608], P(None, 'seq', 'dp')
- table_new: float32 [17, 1152], P(None, 'seq')
- table_copy: bfloat16 [17, 1152], P(None, 'seq')
- table_first_new: float32 [17, 1152], P(None, 'seq')
- table_second_new: float32 [17, 1152], P(None, 'seq')
- down_bias_grad: float32 [1152], P('seq')
The draws below stay inside these ranges and needn't reach their ends.
All inputs are finite; a program needn't handle non-finite values.
Results may differ from the reference program's by a relative error of at most 0.015.
Values may be sent and summed in bfloat16 or wider, within the bound.
A program may use at most 384 MiB of HBM per device.

```python
import math
import jax
import jax.numpy as jnp
from jax import lax

D = 1152
HEADS = 16
FF = 4608
TXT = 120
STEP = 10
HEAD_DIM = 72
LEN = 3072
LATENTS = 4


def feature_ramp(rise_by):
    position = jnp.arange(D, dtype=jnp.float32) / (D - 1)
    return (1.0 + rise_by * position) / (1.0 + 0.5 * rise_by)


def draw_latents(key, part):
    key = jax.random.fold_in(key, 11)
    sample = jnp.clip(jax.random.normal(key, (LATENTS, LEN, D), jnp.float32), -6.0, 6.0)
    return (sample * feature_ramp(2.0)).astype(jnp.bfloat16)


def draw_text_tokens(key, part):
    key = jax.random.fold_in(key, 12)
    sample = jnp.clip(jax.random.normal(key, (LATENTS, TXT, D), jnp.float32), -6.0, 6.0)
    return (sample * feature_ramp(2.0)).astype(jnp.bfloat16)


def draw_cotangent(key, part):
    key = jax.random.fold_in(key, 13)
    sample = jnp.clip(jax.random.normal(key, (LATENTS, LEN, D), jnp.float32), -6.0, 6.0)
    return (sample * feature_ramp(2.0)).astype(jnp.bfloat16)


def draw_w_attn(key, part):
    key = jax.random.fold_in(key, 21)
    fan_in = jnp.array([D, D, D, D // 16, D, D, D, D // 4], jnp.float32)
    sample = jnp.clip(jax.random.normal(key, (8, D, D), jnp.float32), -6.0, 6.0)
    return sample * lax.rsqrt(fan_in)[:, None, None]


def draw_w_mlp(key, part):
    key = jax.random.fold_in(key, 22)
    fan_in = jnp.array([D, FF], jnp.float32)
    sample = jnp.clip(jax.random.normal(key, (2, D, FF), jnp.float32), -6.0, 6.0)
    return sample * lax.rsqrt(fan_in)[:, None, None]


def block_scale(rng, dims, split, low, top_value):
    def one(dim, blocks):
        heights = jax.random.uniform(jax.random.fold_in(jax.random.fold_in(rng, 6), dim), (blocks,), jnp.float32, low / len(split), top_value / len(split))
        return jnp.repeat(jnp.exp(heights), dims[dim] // blocks).reshape((-1,) + (1,) * (len(dims) - dim - 1))

    loudness = one(*split[0])
    for cut in split[1:]:
        loudness = loudness * one(*cut)
    return loudness


def bell_draw(rng, dims, scale, most, shards=(), held_as=jnp.bfloat16):
    values = scale * jax.random.normal(rng, dims, jnp.float32)
    if shards:
        values = values * block_scale(rng, dims, shards, -0.22, 0.18)
    return jnp.clip(values, -most, most).astype(held_as)


def setup_inputs(seed: int = 0) -> dict:
    key_of = jax.random.split(jax.random.key(seed), 14)
    return {
        "latents": draw_latents(jax.random.fold_in(key_of[13], 71), 0),
        "time_embed": bell_draw(key_of[1], (LATENTS, 6, D), 0.5, 3.0, ((0, 4),)),
        "text_tokens": draw_text_tokens(jax.random.fold_in(key_of[13], 71), 0),
        "cotangent": draw_cotangent(jax.random.fold_in(key_of[13], 71), 0),
        "w_attn": draw_w_attn(jax.random.fold_in(key_of[13], 71), 0),
        "w_mlp": draw_w_mlp(jax.random.fold_in(key_of[13], 71), 0),
        "bias_table": bell_draw(key_of[6], (17, D), 0.05, 0.3, ((1, 8),), jnp.float32),
        "attn_first": bell_draw(key_of[7], (8, D, D), (5e-5), 0.0003, ((1, 8), (2, 4)), jnp.float32),
        "attn_second": jnp.clip(jnp.exp(math.log(9.99999993922529e-09) - 1.3862944 * jax.random.uniform(key_of[8], (8, D, D), jnp.float32) ** block_scale(key_of[8], (8, D, D), ((1, 8), (2, 4)), -0.2, 0.2)), 2.4999999848063226e-09, 9.99999993922529e-09),
        "mlp_first": bell_draw(key_of[9], (2, D, FF), (3e-4), 0.0018, ((1, 8), (2, 4)), jnp.float32),
        "mlp_second": jnp.clip(jnp.exp(math.log(3.6000000136482413e-07) - 1.3862944 * jax.random.uniform(key_of[10], (2, D, FF), jnp.float32) ** block_scale(key_of[10], (2, D, FF), ((1, 8), (2, 4)), -0.2, 0.2)), 9.000000034120603e-08, 3.6000000136482413e-07),
        "table_first": bell_draw(key_of[11], (17, D), (6e-4), 0.0036, ((1, 8),), jnp.float32),
        "table_second": jnp.clip(jnp.exp(math.log(1.3999999737279722e-06) - 1.35812346 * jax.random.uniform(key_of[12], (17, D), jnp.float32) ** block_scale(key_of[12], (17, D), ((1, 8),), -0.2, 0.2)), 3.6000000136482413e-07, 1.3999999737279722e-06),
    }


exact_mode = lax.Precision.HIGHEST
norm_eps = 1e-06
clip_norm = 1.0
learn_rate = 0.02
first_decay = 0.5
second_decay = 0.5
adam_eps = 1e-08
weight_decay = 0.01

@jax.custom_vjp
def low(v):
    return lax.optimization_barrier(v.astype(jnp.bfloat16)).astype(jnp.float32)

@jax.custom_vjp
def low_back(v):
    return v

def low_keep(v):
    return (low(v), None)

def low_pass(kept, grad):
    return (grad,)

def back_keep(v):
    return (v, None)

def back_low(kept, grad):
    return (low(grad),)
low.defvjp(low_keep, low_pass)
low_back.defvjp(back_keep, back_low)

def layer_norm(tokens_in):
    center = tokens_in - lax.optimization_barrier(jnp.mean(tokens_in, axis=-1, keepdims=True))
    spread = lax.optimization_barrier(jnp.mean(center * center, axis=-1, keepdims=True))
    return center * lax.rsqrt(spread + norm_eps)

def modulate(tokens_in, shift_row, scale_row):
    return layer_norm(tokens_in) * (1.0 + scale_row) + shift_row

def product(left, right):
    return jnp.dot(left, right, precision=exact_mode)

def split_heads(matrix):
    return matrix.reshape(matrix.shape[0], HEADS, HEAD_DIM).transpose(1, 0, 2)

def head_attention(triple):
    queries, key_rows, value_rows = triple
    scores = low_back(product(queries, key_rows.T) * HEAD_DIM ** (-0.5))
    weights = jax.nn.softmax(scores, axis=-1)
    return product(low(weights), value_rows)

def block_forward(tokens_in, time_row, text_rows, w_attn, w_mlp, bias_table):
    length = tokens_in.shape[0]
    attn_low = low(w_attn)
    mlp_low = low(w_mlp)
    vec_low = low(bias_table)
    modulation = vec_low[0:6] + time_row
    act_in = low(modulate(tokens_in, modulation[0], modulation[1]))
    queries = low_back(low(product(act_in, attn_low[0]) + vec_low[6]))
    key_rows = low_back(low(product(act_in, attn_low[1])))
    value_rows = low_back(low(product(act_in, attn_low[2]) + vec_low[7]))
    heads_out = lax.map(jax.checkpoint(head_attention), (split_heads(queries), split_heads(key_rows), split_heads(value_rows)))
    attended = low_back(low(heads_out.transpose(1, 0, 2).reshape(length, D)))
    branch = low_back(product(attended, attn_low[3]) + vec_low[8])
    first_sum = tokens_in + modulation[2] * branch
    cross_in = low(first_sum)
    cross_q = low_back(low(product(cross_in, attn_low[4]) + vec_low[9]))
    text_k = low_back(low(product(text_rows, attn_low[5])))
    text_v = low_back(low(product(text_rows, attn_low[6]) + vec_low[10]))
    query_three = cross_q.reshape(length, HEADS, HEAD_DIM)
    key_three = text_k.reshape(text_rows.shape[0], HEADS, HEAD_DIM)
    value_three = text_v.reshape(text_rows.shape[0], HEADS, HEAD_DIM)
    cross_scores = low_back(jnp.einsum('lhc,thc->hlt', query_three, key_three, precision=exact_mode) * HEAD_DIM ** (-0.5))
    cross_weights = jax.nn.softmax(cross_scores, axis=-1)
    cross_mix = jnp.einsum('hlt,thc->lhc', low(cross_weights), value_three, precision=exact_mode)
    cross_out = low_back(low(cross_mix.reshape(length, D)))
    cross_branch = low_back(product(cross_out, attn_low[7]) + vec_low[11])
    second_sum = first_sum + cross_branch
    act_mid = low(modulate(second_sum, modulation[3], modulation[4]))
    hidden_pre = low_back(product(act_mid, mlp_low[0]) + vec_low[13:17].reshape(FF))
    hidden = low(jax.nn.gelu(hidden_pre, approximate=True))
    mlp_branch = low_back(product(hidden, mlp_low[1].T) + vec_low[12])
    return second_sum + modulation[5] * mlp_branch

def adam_step(weight, gradient, first_moment, second_moment, factor):
    clipped = gradient * factor
    first_new = first_decay * first_moment + (1.0 - first_decay) * clipped
    second_new = second_decay * second_moment + (1.0 - second_decay) * clipped * clipped
    first_hat = first_new / (1.0 - first_decay ** STEP)
    second_hat = second_new / (1.0 - second_decay ** STEP)
    updated = weight - learn_rate * (first_hat / (jnp.sqrt(second_hat) + adam_eps) + weight_decay * weight)
    return (updated, first_new, second_new)

def reference(latents, time_embed, text_tokens, cotangent, w_attn, w_mlp, bias_table, attn_first, attn_second, mlp_first, mlp_second, table_first, table_second):

    def one_latent(running, latent_item):
        tokens_in, time_row, text_rows, grad_out = latent_item
        result, pullback = jax.vjp(block_forward, tokens_in.astype(jnp.float32), time_row.astype(jnp.float32), text_rows.astype(jnp.float32), w_attn, w_mlp, bias_table)
        gradients = pullback(grad_out.astype(jnp.float32))
        running = (running[0] + gradients[3], running[1] + gradients[4], running[2] + gradients[5])
        return (running, (result.astype(jnp.bfloat16), gradients[0], gradients[1], gradients[2]))
    initial = (jnp.zeros(w_attn.shape, jnp.float32), jnp.zeros(w_mlp.shape, jnp.float32), jnp.zeros(bias_table.shape, jnp.float32))
    grad_sums, stacked = lax.scan(one_latent, initial, (latents, time_embed, text_tokens, cotangent))
    grad_attn, grad_mlp, grad_table = grad_sums
    squares = jnp.sum(grad_attn * grad_attn) + jnp.sum(grad_mlp * grad_mlp) + jnp.sum(grad_table * grad_table)
    grad_norm = jnp.sqrt(squares)
    factor = jnp.minimum(1.0, clip_norm / (grad_norm + 1e-06))
    attn_new, attn_first_new, attn_second_new = adam_step(w_attn, grad_attn, attn_first, attn_second, factor)
    mlp_new, mlp_first_new, mlp_second_new = adam_step(w_mlp, grad_mlp, mlp_first, mlp_second, factor)
    table_new, table_first_new, table_second_new = adam_step(bias_table, grad_table, table_first, table_second, factor)
    return (stacked[0], stacked[1], stacked[2], stacked[3], grad_norm, attn_new, attn_new.astype(jnp.bfloat16), attn_first_new, attn_second_new, mlp_new, mlp_new.astype(jnp.bfloat16), mlp_first_new, mlp_second_new, table_new, table_new.astype(jnp.bfloat16), table_first_new, table_second_new, grad_table[12])
```

```python
import functools
import math

import jax
import jax.numpy as jnp
from jax import lax
from jax.experimental import pallas as pl
from jax.experimental.pallas import tpu as pltpu
from jax.sharding import PartitionSpec as P

STEP = 10

norm_eps = 1e-06
clip_norm = 1.0
learn_rate = 0.02
first_decay = 0.5
second_decay = 0.5
adam_eps = 1e-08
weight_decay = 0.01

HEAD_DIM = 72
MESH = pl.DeviceIdType.MESH
f32 = jnp.float32
bf16 = jnp.bfloat16
MIB = 1 << 20


class Grid:
    def __init__(self, mesh):
        self.np = mesh.shape["dp"]
        self.ns = mesh.shape["seq"]
        root = math.isqrt(self.np)
        self.ax = root if root * root == self.np else self.np
        self.ay = self.np // self.ax
        self.nc = 2 if self.ns % 2 == 0 else 1
        self.nz = self.ns // self.nc
        self.paired = self.nz & (self.nz - 1) == 0

    def here(self):
        p = lax.axis_index("dp")
        s = lax.axis_index("seq")
        return p // self.ax, p % self.ax, s // self.nc, s % self.nc

    def device(self, y, x, z, c):
        return (y * self.ax + x, z * self.nc + c)


def turn(value, step, size):
    return (value + step) % size


class Copies:
    def __init__(self, send_sem, recv_sem, me):
        self.send_sem, self.recv_sem, self.me = send_sem, recv_sem, me
        self.started = []
        self.count = 0

    def make(self, slot, into, src, dst, device):
        return pltpu.make_async_remote_copy(
            src_ref=src,
            dst_ref=dst,
            send_sem=self.send_sem.at[slot],
            recv_sem=self.recv_sem.at[into],
            device_id=device,
            device_id_type=MESH,
        )

    def reserve(self):
        self.count += 1
        return self.count - 1

    def send(self, refs, into=None, when=None):
        slot = self.reserve()
        into = slot if into is None else into
        self.started.append((slot, into, refs, when))

        def start():
            self.make(slot, into, *refs()).start()

        if when is None:
            start()
        else:
            pl.when(when())(start)
        return slot

    def arrived(self, slot, landed):
        self.make(slot, slot, landed, landed, self.me).wait_recv()

    def finish(self):
        for slot, into, refs, when in self.started:

            def done(slot=slot, into=into, refs=refs):
                self.make(slot, into, *refs()).wait_send()

            if when is None:
                done()
            else:
                pl.when(when())(done)


class Local:
    def __init__(self, sems, slot, refs):
        self.sems, self.slot, self.refs = sems, slot, refs
        pltpu.make_async_copy(*refs(), sems.at[slot]).start()

    def wait(self):
        pltpu.make_async_copy(*self.refs(), self.sems.at[self.slot]).wait()


def greet(devices):
    barrier = pltpu.get_barrier_semaphore()
    for device in devices:
        pl.semaphore_signal(barrier, inc=1, device_id=device, device_id_type=MESH)
    pl.semaphore_wait(barrier, len(devices))


def partners(grid, y, x, z, c):
    p, s = grid.device(y, x, z, c)
    found = [(p, turn(s, r, grid.ns)) for r in range(1, grid.ns)]
    found += [(turn(p, r, grid.np), s) for r in range(1, grid.np)]
    return found


def flip_bits(value, r):
    out, bit = value, 1
    while bit <= r:
        if r & bit:
            out = out + bit * (1 - 2 * ((value // bit) % 2))
        bit *= 2
    return out


class Site:
    def __init__(self, grid, send_sem, recv_sem, local_sem):
        self.grid = grid
        self.y, self.x, self.z, self.c = grid.here()
        self.p, self.s = grid.device(self.y, self.x, self.z, self.c)
        self.copies = Copies(send_sem, recv_sem, (self.p, self.s))
        self.local_sem = local_sem
        self.locals = 0
        greet(partners(grid, self.y, self.x, self.z, self.c))

    def local(self, refs):
        self.locals += 1
        return Local(self.local_sem, self.locals - 1, refs)

    def along(self, first_x, r, second=False):
        g = self.grid
        if first_x != second:
            return g.device(self.y, turn(self.x, r, g.ax), self.z, self.c)
        return g.device(turn(self.y, r, g.ay), self.x, self.z, self.c)

    def z_to(self, r):
        return flip_bits(self.z, r) if self.grid.paired else turn(self.z, r, self.grid.nz)

    def z_from(self, r):
        return flip_bits(self.z, r) if self.grid.paired else turn(self.z, self.grid.nz - r, self.grid.nz)

    def z_device(self, r):
        return self.grid.device(self.y, self.x, self.z_to(r), self.c)

    def other_core(self):
        return self.grid.device(self.y, self.x, self.z, 1 - self.c)


def pieces_of(rows, i):
    cut = (rows // 2 + 15) // 16 * 16
    if rows % 16 == 0 and cut < rows:
        return [(0, cut, True), (cut, rows - cut, False)]
    return [(0, rows, i % 2 == 0)]


def sequence(blocks, lead=2):
    steps = []
    for i in range(len(blocks) + 2):
        for ahead in range(lead + 1) if i == 0 else (lead,):
            if i + ahead < len(blocks):
                flow, n = blocks[i + ahead]
                steps.append(("F", i + ahead, functools.partial(flow.first, n)))
        if i < len(blocks):
            flow, n = blocks[i]
            steps.append(("S", i, functools.partial(flow.second, n)))
        if 0 <= i - 1 < len(blocks):
            flow, n = blocks[i - 1]
            steps.append(("T", i - 1, functools.partial(flow.third, n)))
    return steps


def run(steps):
    for _, _, step in steps:
        step()


class ZPhase:
    def __init__(self, site, own_ref, landing):
        self.site, self.own, self.landing = site, own_ref, landing
        self.relay = site.grid.nz == 4
        self.slots = {}

    def inner(self):
        z = self.site.z
        return z * (3 - z) // 2

    def place(self, k):
        t = self.site
        if k == 0:
            return t.z
        if not self.relay:
            return t.z_from(k)
        if k == 1:
            return flip_bits(t.z, 1)
        near = self.inner() if k == 2 else 1 - self.inner()
        return near * (3 - t.z) + (1 - near) * flip_bits(t.z, 2)

    def block(self, k):
        return self.landing(self.place(k))

    def start(self):
        t = self.site
        if not self.relay:
            for k in range(1, t.grid.nz):
                self.slots[k] = t.copies.send(
                    lambda k=k: (self.own, self.landing(t.z), t.z_device(k))
                )
            return
        self.slots[1] = t.copies.send(
            lambda: (self.own, self.landing(t.z), t.z_device(1))
        )
        self.slots[2] = t.copies.reserve()
        self.slots[3] = t.copies.reserve()
        t.copies.send(
            lambda: (self.own, self.landing(t.z), t.z_device(3)),
            self.slots[2],
            lambda: self.inner() == 1,
        )

    def pass_on(self, k):
        if not self.relay:
            return
        t = self.site
        pl.when(self.inner() == 1)(lambda: t.copies.arrived(self.slots[k], self.block(k)))
        t.copies.send(
            lambda: (self.block(k), self.block(k), t.z_device(3 if k == 1 else 1)),
            self.slots[3 if k == 1 else k],
            lambda: self.inner() == 1,
        )

    def settle(self, k):
        def wait():
            self.site.copies.arrived(self.slots[k], self.block(k))

        if self.relay:
            pl.when(self.inner() == 0)(wait)
        else:
            wait()


class GatherFlow:
    def __init__(self, site, out_ref, own_ref):
        self.site, self.out, self.own = site, out_ref, own_ref
        self.rows = out_ref.shape[4]
        self.count = site.grid.nz
        self.zone = ZPhase(site, own_ref, lambda z: self.out.at[site.y, site.x, z, site.c])
        self.slots = {}

    def mine(self, n, piece=None):
        t = self.site
        if piece is None:
            return self.out.at[t.y, t.x, self.zone.place(n), t.c]
        return self.out.at[t.y, t.x, self.zone.place(n), t.c, pl.ds(piece[0], piece[1])]

    def spot(self, n, piece, dy, dx):
        t, g = self.site, self.site.grid
        return self.out.at[
            turn(t.y, g.ay - dy, g.ay),
            turn(t.x, g.ax - dx, g.ax),
            self.zone.place(n),
            t.c,
            pl.ds(piece[0], piece[1]),
        ]

    def plane(self, n, c):
        return self.out.at[:, :, self.zone.place(n), c]

    def start(self):
        self.local = self.site.local(lambda: (self.own, self.mine(0)))

    def first(self, n):
        t, g = self.site, self.site.grid
        if n:
            self.zone.settle(n)

        def refs(piece, first_x, step):
            source = self.own.at[pl.ds(piece[0], piece[1])] if n == 0 else self.mine(n, piece)
            return source, self.mine(n, piece), t.along(first_x, step)

        for piece in pieces_of(self.rows, n):
            for first_x in (piece[2], not piece[2]):
                for step in range(1, g.ax if first_x else g.ay):
                    self.slots["a", n, piece, first_x, step] = t.copies.send(
                        functools.partial(refs, piece, first_x, step)
                    )

    def second(self, n):
        t, g = self.site, self.site.grid
        for piece in pieces_of(self.rows, n):
            first_x = piece[2]
            for step in range(1, g.ax if first_x else g.ay):
                dy, dx = (0, step) if first_x else (step, 0)
                t.copies.arrived(
                    self.slots["a", n, piece, first_x, step], self.spot(n, piece, dy, dx)
                )

                def refs(piece, dy, dx, onward):
                    block = self.spot(n, piece, dy, dx)
                    return block, block, t.along(piece[2], onward, True)

                for onward in range(1, g.ay if first_x else g.ax):
                    self.slots["b", n, piece, step, onward] = t.copies.send(
                        functools.partial(refs, piece, dy, dx, onward)
                    )

    def third(self, n):
        t, g = self.site, self.site.grid
        for piece in pieces_of(self.rows, n):
            first_x = piece[2]
            for onward in range(1, g.ay if first_x else g.ax):
                dy, dx = (onward, 0) if first_x else (0, onward)
                t.copies.arrived(
                    self.slots["a", n, piece, not first_x, onward], self.spot(n, piece, dy, dx)
                )
                for step in range(1, g.ax if first_x else g.ay):
                    dy, dx = (onward, step) if first_x else (step, onward)
                    t.copies.arrived(
                        self.slots["b", n, piece, step, onward], self.spot(n, piece, dy, dx)
                    )
        if n == 0:
            self.local.wait()
        if g.nc > 1:
            self.slots["c", n] = t.copies.send(
                lambda: (self.plane(n, t.c), self.plane(n, t.c), t.other_core())
            )

    def blocks(self):
        return [(self, n) for n in range(self.count)]

    def relays(self):
        return [
            ("P", k, functools.partial(self.zone.pass_on, k)) for k in range(1, self.count)
        ]

    def finish(self):
        t, g = self.site, self.site.grid
        if g.nc > 1:
            for n in range(self.count):
                t.copies.arrived(self.slots["c", n], self.plane(n, 1 - t.c))


def weave(steps, extra):
    found = []
    for step in steps:
        found.append(step)
        found += extra.get(step[:2], [])
    return found


def add_rows(dst, srcs, lo, count):
    chunk = max([n for n in range(16, 49, 16) if count % n == 0], default=count)
    for j in range(count // chunk):
        at = pl.ds(lo + j * chunk, chunk)
        if len(srcs) == 2 and dst.dtype == bf16:
            dst[at] = srcs[0][at] + srcs[1][at]
            continue
        total = srcs[0][at].astype(f32)
        for src in srcs[1:]:
            total = total + src[at].astype(f32)
        dst[at] = total.astype(dst.dtype)


def add_blocks(count, pick, lo, rows):
    def body(i, carry):
        dst, srcs = pick(i)
        add_rows(dst, srcs, lo, rows)
        return carry

    lax.fori_loop(0, count, body, 0)


class ScatterFlow:
    def __init__(self, site, grad_ref, out_ref, mine, half_sum, got_a, got_b, got_z, column_ref=None):
        self.site, self.grad, self.out, self.column = site, grad_ref, out_ref, column_ref
        self.mine, self.half_sum, self.got_a, self.got_b, self.got_z = mine, half_sum, got_a, got_b, got_z
        self.order = list(range(site.grid.nz))[::-1]
        self.slots = {}
        self.locals = {}
        self.base = 0
        self.then = {}
        self.rows = half_sum.shape[3]

    def zone(self, n):
        r = self.order[n]
        return self.site.z_to(r) if r else self.site.z

    def load(self, n):
        t, g = self.site, self.site.grid
        if g.nc > 1:
            self.slots["core", n] = t.copies.send(
                lambda: (
                    self.grad.at[:, :, self.zone(n), 1 - t.c],
                    self.half_sum.at[n],
                    t.other_core(),
                )
            )
        self.locals[n] = t.local(
            lambda: (self.grad.at[:, :, self.zone(n), t.c], self.mine.at[self.spot(n)])
        )

    def own_part(self, n, a, b):
        return self.mine.at[self.spot(n), a, b]

    def spot(self, n):
        return (self.base + n) % self.mine.shape[0]

    def first(self, n):
        t, g = self.site, self.site.grid
        if n in self.locals:
            self.locals[n].wait()
        if g.nc > 1:
            t.copies.arrived(self.slots["core", n], self.half_sum.at[n])

        def pick(i):
            dst = self.half_sum.at[n, i // g.ax, i % g.ax]
            return dst, [self.own_part(n, i // g.ax, i % g.ax)] + ([dst] if g.nc > 1 else [])

        add_blocks(g.ay * g.ax, pick, 0, self.rows)
        if n in self.then:
            self.then[n]()

        def refs(piece, step):
            at = pl.ds(piece[0], piece[1])
            if piece[2]:
                source = self.half_sum.at[n, :, turn(t.x, step, g.ax), at]
            else:
                source = self.half_sum.at[n, turn(t.y, step, g.ay), :, at]
            return source, self.landing(n, piece, step), t.along(piece[2], step)

        for piece in pieces_of(self.rows, n):
            for step in range(1, g.ax if piece[2] else g.ay):
                self.slots["a", n, piece, step] = t.copies.send(
                    functools.partial(refs, piece, step)
                )

    def landing(self, n, piece, step):
        g = self.site.grid
        return self.got_a.at[
            n, step - 1, pl.ds(0, g.ay if piece[2] else g.ax), pl.ds(piece[0], piece[1])
        ]

    def second(self, n):
        t, g = self.site, self.site.grid
        for piece in pieces_of(self.rows, n):
            lo, rows, first_x = piece
            at = pl.ds(lo, rows)
            count, across = (g.ax, g.ay) if first_x else (g.ay, g.ax)
            for step in range(1, count):
                t.copies.arrived(self.slots["a", n, piece, step], self.landing(n, piece, step))

            def pick(i):
                dst = self.half_sum.at[n, i, t.x] if first_x else self.half_sum.at[n, t.y, i]
                return dst, [dst] + [self.got_a.at[n, step - 1, i] for step in range(1, count)]

            add_blocks(across, pick, lo, rows)

            def refs(step, first_x=first_x, at=at):
                if first_x:
                    source = self.half_sum.at[n, turn(t.y, step, g.ay), t.x, at]
                else:
                    source = self.half_sum.at[n, t.y, turn(t.x, step, g.ax), at]
                return source, self.got_b.at[n, step - 1, at], t.along(first_x, step, True)

            for step in range(1, across):
                self.slots["b", n, piece, step] = t.copies.send(functools.partial(refs, step))

    def third(self, n):
        t, g = self.site, self.site.grid
        r = self.order[n]
        own = self.half_sum.at[n, t.y, t.x]
        into = own if self.column is None else self.column.at[r]
        for piece in pieces_of(self.rows, n):
            lo, rows, first_x = piece
            across = g.ay if first_x else g.ax
            for step in range(1, across):
                t.copies.arrived(
                    self.slots["b", n, piece, step], self.got_b.at[n, step - 1, pl.ds(lo, rows)]
                )
            add_rows(into, [own] + [self.got_b.at[n, step - 1] for step in range(1, across)], lo, rows)
        if self.column is None and r:
            self.slots["z", r] = t.copies.send(
                lambda: (self.half_sum.at[n, t.y, t.x], self.got_z.at[r - 1], t.z_device(r))
            )

    def blocks(self):
        return [(self, n) for n in range(len(self.order))]

    def finish(self):
        if self.column is not None:
            return
        t, g = self.site, self.site.grid
        for r in range(1, g.nz):
            t.copies.arrived(self.slots["z", r], self.got_z.at[r - 1])
        own = self.half_sum.at[len(self.order) - 1, t.y, t.x]
        add_rows(
            self.out, [own] + [self.got_z.at[r - 1] for r in range(1, g.nz)], 0, self.rows
        )


class NearScatterFlow(ScatterFlow):
    def load(self, n):
        t = self.site
        if t.grid.nc > 1:
            self.slots["core", n] = t.copies.send(
                lambda: (self.grad.at[n, 1 - t.c], self.half_sum.at[n], t.other_core())
            )

    def own_part(self, n, a, b):
        return self.grad.at[n, self.site.c, a, b]


class ColumnSum:
    def __init__(self, site, column_ref, out_ref, own, got_z):
        self.site, self.column, self.out, self.own, self.got_z = site, column_ref, out_ref, own, got_z
        self.rows = own.shape[0]

    def start(self):
        t = self.site
        self.local = t.local(lambda: (self.column.at[0], self.own))
        self.slots = {
            r: t.copies.send(
                lambda r=r: (self.column.at[r], self.got_z.at[r - 1], t.z_device(r))
            )
            for r in range(1, t.grid.nz)
        }

    def finish(self):
        t = self.site
        self.local.wait()
        for r, slot in self.slots.items():
            t.copies.arrived(slot, self.got_z.at[r - 1])
        add_rows(
            self.out,
            [self.own] + [self.got_z.at[r - 1] for r in range(1, t.grid.nz)],
            0,
            self.rows,
        )


def load_in_turn(blocks):
    depth = blocks[0][0].mine.shape[0]
    for i, (flow, n) in enumerate(blocks):
        if n == 0:
            flow.base = i
    for i, (flow, n) in enumerate(blocks):
        if i < depth:
            flow.load(n)
        if i + depth < len(blocks):
            later, m = blocks[i + depth]
            flow.then[n] = functools.partial(later.load, m)


def scatter_scratch(grid, rows, cols, mine=True):
    block = (rows, cols)
    widest = max(grid.ax, grid.ay)
    depth = 3 if grid.nz <= 4 else 2
    found = [pltpu.VMEM((depth, grid.ay, grid.ax) + block, bf16)] if mine else []
    return found + [
        pltpu.VMEM((grid.nz, grid.ay, grid.ax) + block, bf16),
        pltpu.VMEM((grid.nz, max(1, widest - 1), widest) + block, bf16),
        pltpu.VMEM((grid.nz, max(1, widest - 1)) + block, bf16),
        pltpu.VMEM((max(1, grid.nz - 1),) + block, bf16),
    ]


def by_distance(size):
    return sorted(range(1, size), key=lambda r: (min(r, size - r), r))


class ExchangeFlow:
    def __init__(self, site, in_ref, out_ref, head=None, part=None):
        self.site, self.src, self.dst = site, in_ref, out_ref
        self.index = () if head is None else (head,) if part is None else (head, part)
        self.slots = {}

    def at(self, ref, n):
        return ref.at[(n,) + self.index]

    def start_one(self, r):
        t, ns = self.site, self.site.grid.ns
        if r == 0:
            self.own = t.local(lambda: (self.at(self.src, t.s), self.at(self.dst, t.s)))
            return
        self.slots[r] = t.copies.send(
            lambda: (
                self.at(self.src, turn(t.s, r, ns)),
                self.at(self.dst, t.s),
                (t.p, turn(t.s, r, ns)),
            )
        )

    def start(self):
        for r in by_distance(self.site.grid.ns)[::-1] + [0]:
            self.start_one(r)

    def finish(self):
        t, ns = self.site, self.site.grid.ns
        self.own.wait()
        for r, slot in self.slots.items():
            t.copies.arrived(slot, self.at(self.dst, turn(t.s, ns - r, ns)))


class SpreadFlow:
    def __init__(self, site, in_ref, out_ref, over_dp=False):
        self.site, self.src, self.dst, self.over_dp = site, in_ref, out_ref, over_dp
        g = site.grid
        self.size, self.place = (g.np, site.p) if over_dp else (g.ns, site.s)

    def start(self):
        t = self.site

        def refs(r):
            to = turn(self.place, r, self.size)
            return self.src, self.dst.at[self.place], (to, t.s) if self.over_dp else (t.p, to)

        self.slots = {
            r: t.copies.send(functools.partial(refs, r)) for r in by_distance(self.size)
        }
        self.own = t.local(lambda: (self.src, self.dst.at[self.place]))

    def finish(self):
        self.own.wait()
        for r, slot in self.slots.items():
            self.site.copies.arrived(slot, self.dst.at[turn(self.place, self.size - r, self.size)])


def flip(block):
    return jnp.transpose(block.astype(f32))


def attend_head(qkv, head, keys, values):
    sources, rows = qkv.shape[0], qkv.shape[-1]
    for s in range(sources):
        at = slice(s * rows, (s + 1) * rows)
        keys[:, at] = qkv[s, head, 1]
        values[at, :] = flip(qkv[s, head, 2]).astype(bf16)


def attend_block(scale, qkv, head, block, out, wide, logs, keys, values, scores):
    sources, rows = qkv.shape[0], qkv.shape[-1]
    query = flip(qkv[block, head, 0]).astype(bf16)
    factor = scale * math.log2(math.e)
    peak = None
    for s in range(sources):
        at = slice(s * rows, (s + 1) * rows)
        part = jnp.dot(query, keys[:, at], preferred_element_type=f32)
        scores[:, at] = part
        top = jnp.max(part, axis=-1, keepdims=True)
        peak = top if peak is None else jnp.maximum(peak, top)
    peak = peak * factor
    total = jnp.zeros((rows, 1), f32)
    mixed = jnp.zeros((rows, HEAD_DIM), f32)
    for s in range(sources):
        at = slice(s * rows, (s + 1) * rows)
        part = jnp.exp2(scores[:, at] * factor - peak)
        total = total + jnp.sum(part, axis=-1, keepdims=True)
        mixed = mixed + jnp.dot(part.astype(bf16), values[at, :], preferred_element_type=f32)
    mixed = jnp.transpose(mixed / total)
    wide[head, block] = mixed
    out[block, head] = mixed.astype(bf16)
    logs[head, block] = jnp.transpose(jnp.broadcast_to(peak + jnp.log2(total), (rows, 8)))


def attend_scratch(qkv):
    sources, _, _, dim, rows = qkv.shape
    length = sources * rows
    return [
        pltpu.VMEM((dim, length), bf16),
        pltpu.VMEM((length, dim), bf16),
        pltpu.VMEM((rows, length), f32),
    ]


def attend_back_head(qkv, head, keys, key_rows, values, grad_k, grad_v):
    sources, rows = qkv.shape[0], qkv.shape[-1]
    for s in range(sources):
        at = slice(s * rows, (s + 1) * rows)
        keys[:, at] = qkv[s, head, 1]
        key_rows[at, :] = flip(qkv[s, head, 1]).astype(bf16)
        values[:, at] = qkv[s, head, 2]
    grad_k[...] = jnp.zeros_like(grad_k)
    grad_v[...] = jnp.zeros_like(grad_v)


def attend_back_block(
    scale, qkv, grad_in, wide, logs, head, block, out, keys, key_rows, values, grad_k, grad_v
):
    sources, rows = qkv.shape[0], qkv.shape[-1]
    query_t = qkv[block, head, 0]
    grad_t = grad_in[block, head]
    query = flip(query_t).astype(bf16)
    grad = flip(grad_t).astype(bf16)
    factor = scale * math.log2(math.e)
    inner = jnp.sum(grad_t.astype(f32) * wide[head, block], axis=0, keepdims=True)
    inner = jnp.transpose(jnp.broadcast_to(inner, (8, rows)))[:, 0:1]
    log_rows = jnp.transpose(logs[head, block])[:, 0:1]
    grad_q = jnp.zeros((rows, HEAD_DIM), f32)
    for s in range(sources):
        at = slice(s * rows, (s + 1) * rows)
        part = jnp.dot(query, keys[:, at], preferred_element_type=f32)
        probs = jnp.exp2(part * factor - log_rows)
        grad_p = jnp.dot(grad, values[:, at], preferred_element_type=f32)
        grad_s = (probs * (grad_p - inner)).astype(bf16)
        grad_q = grad_q + jnp.dot(grad_s, key_rows[at, :], preferred_element_type=f32)
        grad_k[:, at] += jnp.dot(query_t, grad_s, preferred_element_type=f32)
        grad_v[:, at] += jnp.dot(grad_t, probs.astype(bf16), preferred_element_type=f32)
    out[block, head, 0] = jnp.transpose(grad_q * scale).astype(bf16)


def attend_back_end(scale, head, out, grad_k, grad_v):
    sources, rows = out.shape[0], out.shape[-1]
    for s in range(sources):
        at = slice(s * rows, (s + 1) * rows)
        out[s, head, 1] = (grad_k[:, at] * scale).astype(bf16)
        out[s, head, 2] = grad_v[:, at].astype(bf16)


def attend_back_scratch(qkv):
    sources, _, _, dim, rows = qkv.shape
    length = sources * rows
    return [
        pltpu.VMEM((dim, length), bf16),
        pltpu.VMEM((length, dim), bf16),
        pltpu.VMEM((dim, length), bf16),
        pltpu.VMEM((dim, length), f32),
        pltpu.VMEM((dim, length), f32),
    ]


VMEM = pl.BlockSpec(memory_space=pltpu.VMEM)
HBM = pl.BlockSpec(memory_space=pltpu.HBM)


def gather_shape(grid, rows, cols):
    return jax.ShapeDtypeStruct((grid.ay, grid.ax, grid.nz, grid.nc, rows, cols), bf16)


def gather_slots(grid):
    across = 2 * (grid.ax + grid.ay - 2) + 2 * (grid.ax - 1) * (grid.ay - 1)
    return grid.nz + 6 + grid.nz * (across + 1)


def scatter_slots(grid):
    return grid.nz * (2 * (grid.ax + grid.ay - 2) + 1) + grid.nz - 1


def move(grid, kernel, name, slots, locals_, call_id, out_shape, out_specs, in_specs, scratch, args, vmem, cost=None):
    return pl.pallas_call(
        functools.partial(kernel, grid),
        name=name,
        out_shape=out_shape,
        in_specs=in_specs,
        out_specs=out_specs,
        scratch_shapes=list(scratch)
        + [
            pltpu.SemaphoreType.DMA((slots,)),
            pltpu.SemaphoreType.DMA((slots,)),
            pltpu.SemaphoreType.DMA((locals_,)),
        ],
        compiler_params=pltpu.CompilerParams(
            collective_id=call_id, has_side_effects=True, vmem_limit_bytes=vmem * MIB
        ),
        cost_estimate=cost,
    )(*args)


def planned(steps, times, when):
    inside, rest = [], []
    at = 0
    for kind, n, step in steps:
        while at < len(times) and times[at] < when(kind, n):
            at += 1
        if at < len(times):
            inside.append((at, step))
        else:
            rest.append((kind, n, step))
    return inside, rest


def attention_kernel(
    grid,
    scale,
    own_0,
    own_a,
    own_b,
    own_c,
    table_ref,
    time_ref,
    lat,
    text,
    out_0,
    out_a,
    out_b,
    out_c,
    back_ref,
    qkv,
    wide,
    logs,
    a1,
    biases,
    z1,
    x2,
    c1,
    cq,
    ck,
    cv,
    oc,
    a2,
    *refs,
):
    mixed, keys, values, scores, table_all, parts, weights, att, sems = refs[:9]
    site = Site(grid, *refs[9:])
    heads, sources = qkv.shape[1], qkv.shape[0]
    tokens, width = a1.shape
    cols = weights.shape[4]
    cw = cols // 4
    rows = own_0.shape[0]
    nz, nc = grid.nz, grid.nc
    flows = [
        GatherFlow(site, out, own)
        for out, own in ((out_0, own_0), (out_a, own_a), (out_b, own_b), (out_c, own_c))
    ]
    incoming = [ExchangeFlow(site, parts, qkv, h) for h in range(heads)]
    outgoing = [ExchangeFlow(site, mixed, back_ref, h) for h in range(heads)]
    table = SpreadFlow(site, table_ref, table_all)
    table.start()
    flows[0].start()
    flows[0].zone.start()
    flows[0].first(0)
    for flow in flows[1:]:
        flow.start()
    relays = [flow.relays() for flow in flows]
    zones = [[("Z", k, flow.zone.start)] for k, flow in enumerate(flows)]
    steps = weave(
        sequence([block for flow in flows for block in flow.blocks()]),
        {
            ("F", 0): relays[0][:1],
            ("F", 1): relays[0][1:2],
            ("S", 0): relays[0][2:] + zones[1],
            ("S", 1): relays[1][:1],
            ("F", 3): relays[1][1:2],
            ("S", 2): relays[1][2:] + zones[2],
            ("S", 3): relays[2][:1],
            ("F", 5): relays[2][1:2],
            ("S", 4): relays[2][2:],
        },
    )[1:]

    normed, _ = norm_parts(lat[...].astype(f32))
    table.finish()
    part = table_ref.shape[1]
    for n in range(grid.ns):
        biases[:, n * part : (n + 1) * part] = table_all[n].astype(f32)
    shift = biases[0:1, :] + time_ref[0:1, :].astype(f32)
    gain = 1.0 + biases[1:2, :] + time_ref[1:2, :].astype(f32)
    a1[...] = (normed * gain + shift).astype(bf16)

    cut = max(i for i, (kind, n, _) in enumerate(steps) if kind == "T" and n == nz - 1) + 1
    run(steps[:cut])
    flows[0].finish()

    order = [(out, p) for out in (out_0, out_0, out_a, out_a) for p in range(grid.np)]

    def load(k):
        out, p = order[k]
        return pltpu.make_async_copy(
            out.at[p // grid.ax, p % grid.ax], weights.at[k % 2], sems.at[k % 2]
        )

    def through(left, k, lo, hi):
        slot = weights.at[k % 2]
        if rows % 16 == 0:
            return dot(left[...], slot[:, :, :, lo:hi].reshape(width, hi - lo))
        found = None
        for n in range(nz * nc):
            piece = dot(left[:, n * rows : (n + 1) * rows], slot[n // nc, n % nc, :, lo:hi])
            found = piece if found is None else found + piece
        return found

    def used(k):
        if k + 2 < len(order):
            load(k + 2).start()

    load(0).start()
    load(1).start()
    for p in range(grid.np):
        load(p).wait()
        found = through(a1, p, 0, 3 * cw)
        used(p)
        found = jnp.transpose(found)
        at = slice(p * cw, (p + 1) * cw)
        rows_q = jnp.transpose(jnp.broadcast_to(biases[6:7, at], (8, cw)))[:, 0:1]
        rows_v = jnp.transpose(jnp.broadcast_to(biases[7:8, at], (8, cw)))[:, 0:1]
        thirds = (found[0:cw] + rows_q, found[cw : 2 * cw], found[2 * cw : 3 * cw] + rows_v)
        for h in range(cw // HEAD_DIM):
            device, head = divmod(p * (cw // HEAD_DIM) + h, heads)
            for j in range(3):
                parts[device, head, j] = thirds[j][h * HEAD_DIM : (h + 1) * HEAD_DIM].astype(bf16)
    incoming[0].start()

    def due(kind, n):
        return 11.5 * n + {"F": -6, "S": 12, "T": 24, "P": 0, "Z": 0}[kind]

    cut_b = max([i + 1 for i, (kind, n, _) in enumerate(steps) if due(kind, n) <= 86] + [cut])
    run(steps[cut:cut_b])
    incoming[0].finish()
    for flow in incoming[1:2]:
        flow.start()
    times = [92 + 29 * (i // sources) + 2.4 * (i % sources) for i in range(heads * sources)]
    inside, rest = planned(steps[cut_b:], times, due)
    for n, (_, _, step) in enumerate(zones[3] + relays[3]):
        inside.append(((heads - 1) * sources + min(2 * n, sources - 1), step))

    def turn_of(i, carry):
        head, block = i // sources, turn(site.s, i, sources)
        for h in range(1, heads):

            @pl.when(i == h * sources)
            def _():
                incoming[h].finish()
                for flow in incoming[h + 1 : h + 2]:
                    flow.start()

        @pl.when(i % sources == 0)
        def _():
            attend_head(qkv, head, keys, values)

        attend_block(scale, qkv, head, block, mixed, wide, logs, keys, values, scores)
        for h in range(heads):
            for r in range(sources):
                pl.when(i == h * sources + r)(functools.partial(outgoing[h].start_one, r))
        for at in sorted({n for n, _ in inside}):

            @pl.when(i == at)
            def _():
                for n, step in inside:
                    if n == at:
                        step()

        return carry

    lax.fori_loop(0, heads * sources, turn_of, 0)

    def advance(count):
        run(rest[:count])
        del rest[:count]

    def vector(n):
        return biases[n : n + 1, :] + time_ref[n : n + 1, :].astype(f32)

    advance(max([i + 1 for i, (_, n, _) in enumerate(rest) if n < 2 * nz] + [0]))
    flows[1].finish()
    for flow in outgoing:
        flow.finish()
    for n in range(sources * heads):
        at = slice(n * HEAD_DIM, (n + 1) * HEAD_DIM)
        att[:, at] = flip(back_ref[n // heads, n % heads]).astype(bf16)
    k = grid.np
    for p in range(grid.np):
        at = slice(p * cw, (p + 1) * cw)
        load(k + p).wait()
        z1[:, at] = through(att, k + p, 3 * cw, 4 * cw) + biases[8:9, at]
        used(k + p)
    advance(2)
    x1 = lat[...].astype(f32) + vector(2) * z1[...]
    x2[...] = x1
    c1[...] = x1.astype(bf16)
    k += grid.np
    for p in range(grid.np):
        at = slice(p * cw, (p + 1) * cw)
        load(k + p).wait()
        ck[:, at] = through(text, k + p, cw, 2 * cw).astype(bf16)
        cv[:, at] = (through(text, k + p, 2 * cw, 3 * cw) + biases[10:11, at]).astype(bf16)
        cq[:, at] = (through(c1, k + p, 0, cw) + biases[9:10, at]).astype(bf16)
        used(k + p)
    advance(2)
    for h in range(width // HEAD_DIM):
        at = slice(h * HEAD_DIM, (h + 1) * HEAD_DIM)
        probs = cross_probs(scale, cq[:, at], ck[:, at])
        oc[:, at] = dot(probs.astype(bf16), cv[:, at]).astype(bf16)
        if h == width // HEAD_DIM // 2:
            advance(2)
    advance(2)
    k += grid.np
    for p in range(grid.np):
        at = slice(p * cw, (p + 1) * cw)
        load(k + p).wait()
        x2[:, at] = x2[:, at] + through(oc, k + p, 3 * cw, 4 * cw) + biases[11:12, at]
        used(k + p)
    normed, _ = norm_parts(x2[...])
    a2[...] = (normed * (1.0 + vector(4)) + vector(3)).astype(bf16)
    advance(len(rest))
    for flow in flows[2:]:
        flow.finish()
    site.copies.finish()


def attention(grid, scale, owns, table, time, lat, text):
    rows, cols = owns[0].shape
    tokens, width = lat.shape
    sources = grid.ns
    heads = width // HEAD_DIM // sources
    length = sources * tokens
    blocks = jax.ShapeDtypeStruct((sources, heads, 3, HEAD_DIM, tokens), bf16)
    low = jax.ShapeDtypeStruct((tokens, width), bf16)
    high = jax.ShapeDtypeStruct((tokens, width), f32)
    word = jax.ShapeDtypeStruct(text.shape, bf16)
    return move(
        grid,
        lambda g, *refs: attention_kernel(g, scale, *refs),
        "attention",
        4 * gather_slots(grid) + 2 * grid.ns * heads + grid.ns,
        5 + 2 * heads,
        1,
        [gather_shape(grid, rows, cols)] * 4
        + [
            jax.ShapeDtypeStruct((sources, heads, HEAD_DIM, tokens), bf16),
            blocks,
            jax.ShapeDtypeStruct((heads, sources, HEAD_DIM, tokens), f32),
            jax.ShapeDtypeStruct((heads, sources, 8, tokens), f32),
            jax.ShapeDtypeStruct((tokens, width), bf16),
            jax.ShapeDtypeStruct((table.shape[0], width), f32),
            high,
            high,
            low,
            low,
            word,
            word,
            low,
            low,
        ],
        [HBM] * 4 + [VMEM] * 14,
        [HBM] * 4 + [VMEM] * 4,
        [pltpu.VMEM((sources, heads, HEAD_DIM, tokens), bf16)]
        + attend_scratch(blocks)
        + [
            pltpu.VMEM((grid.ns,) + table.shape, bf16),
            pltpu.VMEM(blocks.shape, bf16),
            pltpu.VMEM((2, grid.nz, grid.nc, rows, cols), bf16),
            pltpu.VMEM((tokens, width), bf16),
            pltpu.SemaphoreType.DMA((2,)),
        ],
        owns + (table, time, lat, text),
        56,
        pl.CostEstimate(
            flops=4 * heads * length * length * HEAD_DIM,
            bytes_accessed=60 * MIB,
            transcendentals=heads * length * length,
        ),
    )


def attention_back_kernel(
    grid,
    scale,
    grad_a,
    grad_b,
    in_ref,
    text_ref,
    qkv,
    wide,
    logs,
    own_ref,
    column_ref,
    back_ref,
    words_ref,
    *refs,
):
    scratch_a, scratch_b = refs[:5], refs[5:9]
    refs = refs[9:]
    text_got, text_low, grad_in, grad_qkv, keys, key_rows, values, grad_k, grad_v = refs[:9]
    site = Site(grid, *refs[9:])
    heads, sources = qkv.shape[1], qkv.shape[0]
    incoming = [ExchangeFlow(site, in_ref, grad_in, h) for h in range(heads)]
    text = ExchangeFlow(site, text_ref, text_got)
    queries = [ExchangeFlow(site, grad_qkv, back_ref, h, 0) for h in range(heads)]
    outgoing = [ExchangeFlow(site, grad_qkv, back_ref, h, pl.ds(1, 2)) for h in range(heads)]
    mine = scratch_a[0]
    a = ScatterFlow(site, grad_a, own_ref.at[0], *scratch_a)
    b = ScatterFlow(site, grad_b, None, mine, *scratch_b, column_ref=column_ref)
    blocks = a.blocks() + b.blocks()
    incoming[0].start()
    load_in_turn(blocks)
    steps = sequence(blocks)

    def due(kind, n):
        return 11.5 * n + {"F": 4, "S": 18, "T": 30}[kind]

    cut = max(i for i, (kind, n, _) in enumerate(steps) if due(kind, n) <= 10) + 1
    run(steps[:cut])
    incoming[0].finish()
    for flow in incoming[1:]:
        flow.start()
    text.start()
    times = [14 + 4.6 * i for i in range(heads * sources)]
    inside, rest = planned(steps[cut:], times, due)
    words = SpreadFlow(site, text_low, words_ref)

    def sum_text():
        text.finish()
        total = text_got[0].astype(f32)
        for n in range(1, grid.ns):
            total = total + text_got[n].astype(f32)
        text_low[...] = total.astype(bf16)
        words.start()

    inside.append((sources - 1, sum_text))

    def turn_of(i, carry):
        head, block = i // sources, turn(site.s, i, sources)
        for h in range(1, heads):
            pl.when(i == h * sources)(incoming[h].finish)

        @pl.when(i % sources == 0)
        def _():
            attend_back_head(qkv, head, keys, key_rows, values, grad_k, grad_v)

        attend_back_block(
            scale, qkv, grad_in, wide, logs, head, block, grad_qkv, keys, key_rows, values, grad_k, grad_v
        )

        @pl.when(i % sources == sources - 1)
        def _():
            attend_back_end(scale, head, grad_qkv, grad_k, grad_v)

        for h in range(heads):
            for r in range(sources):
                pl.when(i == h * sources + r)(functools.partial(queries[h].start_one, r))
            pl.when(i == (h + 1) * sources - 1)(outgoing[h].start)
        for at in sorted({n for n, _ in inside}):

            @pl.when(i == at)
            def _():
                for n, step in inside:
                    if n == at:
                        step()

        return carry

    lax.fori_loop(0, heads * sources, turn_of, 0)
    run(rest)
    for flow in [a, b, words] + queries + outgoing:
        flow.finish()
    site.copies.finish()


def attention_back(grid, scale, grads, blocks, text, qkv, wide, logs, rows, cols):
    shape = (grid.ay, grid.ax, grid.nz, grid.nc, rows, cols)
    sources, heads, _, dim, tokens = qkv.shape
    length = sources * tokens
    return move(
        grid,
        lambda g, *refs: attention_back_kernel(g, scale, *refs),
        "attention_back",
        2 * scatter_slots(grid) + grid.ns * (2 + 3 * heads),
        2 * grid.nz + 2 + 3 * heads,
        2,
        [
            jax.ShapeDtypeStruct((1, rows, cols), f32),
            jax.ShapeDtypeStruct((grid.nz, rows, cols), bf16),
            jax.ShapeDtypeStruct(qkv.shape, bf16),
            jax.ShapeDtypeStruct(text.shape, bf16),
        ],
        [VMEM, VMEM, HBM, HBM],
        [HBM] * 4 + [VMEM] * 3,
        scatter_scratch(grid, rows, cols)
        + scatter_scratch(grid, rows, cols, mine=False)
        + [
            pltpu.VMEM(text.shape, bf16),
            pltpu.VMEM(text.shape[1:], bf16),
            pltpu.VMEM((sources, heads, dim, tokens), bf16),
            pltpu.VMEM(qkv.shape, bf16),
        ]
        + attend_back_scratch(qkv),
        tuple(g.reshape(shape) for g in grads) + (blocks, text, qkv, wide, logs),
        60,
        pl.CostEstimate(
            flops=10 * heads * length * length * dim,
            bytes_accessed=60 * MIB,
            transcendentals=heads * length * length,
        ),
    )


def dot(left, right, kind="nn"):
    contract = ((0 if kind[0] == "t" else 1,), (1 if kind[1] == "t" else 0,))
    return lax.dot_general(left, right, (contract, ((), ())), preferred_element_type=f32)


def norm_parts(tokens_in):
    center = tokens_in - jnp.mean(tokens_in, axis=-1, keepdims=True)
    spread = jnp.mean(center * center, axis=-1, keepdims=True)
    rate = lax.rsqrt(spread + norm_eps)
    return center * rate, rate


def norm_back(grad, normed, rate, gain):
    inner = grad * gain
    mean = jnp.mean(inner, axis=-1, keepdims=True)
    along = jnp.mean(inner * normed, axis=-1, keepdims=True)
    return rate * (inner - mean - normed * along)


def column(rows_ref, n):
    return rows_ref[n : n + 1, :]


def cross_probs(scale, query, keys):
    scores = dot(query, keys, "nt") * scale
    part = jnp.exp(scores - jnp.max(scores, axis=-1, keepdims=True))
    return part / jnp.sum(part, axis=-1, keepdims=True)


def gelu_pair(pre):
    rate = math.sqrt(2.0 / math.pi)
    square = pre * pre
    bend = jnp.tanh(rate * pre * (1.0 + 0.044715 * square))
    half = 0.5 * (1.0 + bend)
    slope = half + 0.5 * pre * (1.0 - bend * bend) * rate * (1.0 + 3 * 0.044715 * square)
    return pre * half, slope


def mlp_kernel(
    a2, cot, x2, up, down, b1, rows_ref, out, da2, grad_up, grad_down, du_sum, sums, a2_t, dz3, dz3_t, z3
):
    p = pl.program_id(0)

    @pl.when(p == 0)
    def _():
        back = (column(rows_ref, 0) * cot[...].astype(f32)).astype(bf16)
        dz3[...] = back
        dz3_t[...] = flip(back).astype(bf16)
        a2_t[...] = flip(a2[...]).astype(bf16)
        sums[0:1, :] = jnp.sum(back.astype(f32), axis=0, keepdims=True)

    pre = dot(a2[...], up[0]) + b1[0]
    act, slope = gelu_pair(pre)
    hidden = act.astype(bf16)
    grad = (dot(dz3[...], down[0]) * slope).astype(bf16)
    du_sum[0] = jnp.sum(grad.astype(f32), axis=0, keepdims=True)
    part = dot(hidden, down[0], "nt")
    back = dot(grad, up[0], "nt")

    @pl.when(p == 0)
    def _():
        z3[...] = part
        da2[...] = back

    @pl.when(p > 0)
    def _():
        z3[...] += part
        da2[...] += back

    grad_up[0] = dot(a2_t[...], grad).astype(bf16)
    grad_down[0] = dot(dz3_t[...], hidden).astype(bf16)

    @pl.when(p == pl.num_programs(0) - 1)
    def _():
        branch = z3[...] + column(rows_ref, 1)
        out[...] = (x2[...] + column(rows_ref, 0) * branch).astype(bf16)
        sums[1:2, :] = jnp.sum(cot[...].astype(f32) * branch, axis=0, keepdims=True)


def mlp(a2, cot, x2, up, down, b1, rows):
    tokens, width = a2.shape
    np_, _, cols = up.shape
    block = pl.BlockSpec((1, width, cols), lambda p: (p, 0, 0))
    row = pl.BlockSpec((1, 1, cols), lambda p: (p, 0, 0))
    return pl.pallas_call(
        mlp_kernel,
        name="mlp",
        grid=(np_,),
        out_shape=[
            jax.ShapeDtypeStruct((tokens, width), bf16),
            jax.ShapeDtypeStruct((tokens, width), f32),
            jax.ShapeDtypeStruct(up.shape, bf16),
            jax.ShapeDtypeStruct(down.shape, bf16),
            jax.ShapeDtypeStruct((np_, 1, cols), f32),
            jax.ShapeDtypeStruct((8, width), f32),
        ],
        in_specs=[VMEM, VMEM, VMEM, block, block, row, VMEM],
        out_specs=[VMEM, VMEM, block, block, row, VMEM],
        scratch_shapes=[
            pltpu.VMEM((width, tokens), bf16),
            pltpu.VMEM((tokens, width), bf16),
            pltpu.VMEM((width, tokens), bf16),
            pltpu.VMEM((tokens, width), f32),
        ],
        compiler_params=pltpu.CompilerParams(vmem_limit_bytes=56 * MIB),
        cost_estimate=pl.CostEstimate(
            flops=12 * tokens * width * cols * np_,
            bytes_accessed=44 * MIB,
            transcendentals=tokens * cols * np_,
        ),
    )(a2, cot, x2, up, down, b1, rows)


def cross_back_kernel(
    grid,
    scale,
    da2,
    x2,
    cot,
    z1,
    cq,
    ck,
    cv,
    c1,
    oc,
    text,
    rows_ref,
    w_self,
    w_cross,
    grad_ref,
    dx1,
    do_t,
    dz1,
    text_part,
    sums,
    own_ref,
    grad_cross,
    *refs,
):
    scratch, refs = refs[:5], refs[5:]
    doc, dz2, dcq, part_k, part_v, left, wo, wc, stage, sems = refs[:10]
    low = doc
    np_, width, wide = w_self.shape
    cw = wide // 4
    lo = 3 * cw // 128 * 128
    load_o = pltpu.make_async_copy(w_self.at[:, :, pl.ds(lo, wide - lo)], wo, sems.at[0])
    load_c = pltpu.make_async_copy(w_cross, wc, sems.at[1])
    load_c.start()
    load_o.start()
    site = Site(grid, *refs[10:])
    flow = ScatterFlow(site, grad_ref, own_ref.at[0], *scratch)
    load_in_turn(flow.blocks())
    steps = sequence(flow.blocks())

    def advance(count):
        run(steps[:count])
        del steps[:count]

    def total(n, matrix):
        sums[n : n + 1, :] = jnp.sum(matrix, axis=0, keepdims=True)

    normed, rate = norm_parts(x2[...])
    grad = da2[...]
    total(0, grad)
    total(1, grad * normed)
    grad = cot[...].astype(f32) + norm_back(grad, normed, rate, 1.0 + column(rows_ref, 0))
    dx1[...] = grad
    dz2[...] = grad.astype(bf16)
    total(2, dz2[...].astype(f32))
    advance(2)
    load_c.wait()

    def back(source, w, first):
        found = None
        for p in range(np_):
            part = dot(source[:, p * cw : (p + 1) * cw], w[p, :, first : first + cw], "nt")
            found = part if found is None else found + part
        return found

    doc[...] = back(dz2, wc, 3 * cw).astype(bf16)
    advance(1)
    half = width // HEAD_DIM // 2
    for h in range(width // HEAD_DIM):
        at = slice(h * HEAD_DIM, (h + 1) * HEAD_DIM)
        query, keys, grad_h = cq[:, at], ck[:, at], doc[:, at]
        probs = cross_probs(scale, query, keys)
        grad_p = dot(grad_h, cv[:, at], "nt")
        inner = jnp.sum(grad_p * probs, axis=-1, keepdims=True)
        grad_s = (probs * (grad_p - inner)).astype(bf16)
        dcq[:, at] = (dot(grad_s, keys) * scale).astype(bf16)
        part_k[:, at] = (dot(grad_s, query, "tn") * scale).astype(bf16)
        whole = dot(probs.astype(bf16), grad_h, "tn")
        part_v[:, at] = whole.astype(bf16)
        sums[4:5, at] = jnp.sum(whole, axis=0, keepdims=True)
        if h == half:
            advance(2)
    total(3, dcq[...].astype(f32))
    advance(2)
    grad = dx1[...] + back(dcq, wc, 0)
    dx1[...] = grad
    total(5, grad * z1[...])
    low[...] = (column(rows_ref, 1) * grad).astype(bf16)
    total(6, low[...].astype(f32))
    for p in range(np_):
        dz1[p] = low[:, p * cw : (p + 1) * cw]
    load_o.wait()
    do_t[...] = jnp.transpose(back(low, wo, 3 * cw - lo)).astype(bf16)
    advance(1)
    words = ck.shape[0]
    text_part[...] = jnp.zeros_like(text_part)
    text_part[0:words, 0:width] = part_k[...]
    text_part[0:words, width : 2 * width] = part_v[...]
    left[0] = flip(c1[...]).astype(bf16)
    left[1] = flip(oc[...]).astype(bf16)
    words_t = flip(text[...]).astype(bf16)

    def store(p):
        return pltpu.make_async_copy(stage.at[p % 2], grad_cross.at[p], sems.at[2 + p % 2])

    for p in range(np_):
        at = slice(p * cw, (p + 1) * cw)
        if p >= 2:
            store(p - 2).wait()
        into = stage.at[p % 2]
        into[:, 0:cw] = dot(left[0], dcq[:, at]).astype(bf16)
        into[:, cw : 2 * cw] = dot(words_t, part_k[:, at]).astype(bf16)
        into[:, 2 * cw : 3 * cw] = dot(words_t, part_v[:, at]).astype(bf16)
        into[:, 3 * cw : 4 * cw] = dot(left[1], dz2[:, at]).astype(bf16)
        store(p).start()
        if p % (np_ // 4 if np_ >= 4 else 1) == 0:
            advance(1)
    advance(len(steps))
    for p in range(max(0, np_ - 2), np_):
        store(p).wait()
    flow.finish()
    site.copies.finish()


def cross_backward(grid, scale, da2, x2, cot, z1, cq, ck, cv, c1, oc, text, rows, w_self, w_cross, grad, rows_padded, own_rows):
    tokens, width = x2.shape
    np_, _, wide = w_self.shape
    words = ck.shape[0]
    lo = 3 * (wide // 4) // 128 * 128
    low = pltpu.VMEM((tokens, width), bf16)
    word = pltpu.VMEM((words, width), bf16)
    return move(
        grid,
        lambda g, *refs: cross_back_kernel(g, scale, *refs),
        "cross_backward",
        scatter_slots(grid),
        grid.nz,
        5,
        [
            jax.ShapeDtypeStruct((tokens, width), f32),
            jax.ShapeDtypeStruct((width, tokens), bf16),
            jax.ShapeDtypeStruct((np_, tokens, wide // 4), bf16),
            jax.ShapeDtypeStruct((rows_padded, 2 * width), bf16),
            jax.ShapeDtypeStruct((8, width), f32),
            jax.ShapeDtypeStruct((1, own_rows, wide), f32),
            jax.ShapeDtypeStruct(w_cross.shape, bf16),
        ],
        [VMEM] * 6 + [HBM],
        [VMEM] * 11 + [HBM] * 3,
        scatter_scratch(grid, own_rows, wide)
        + [
            low,
            low,
            low,
            word,
            word,
            pltpu.VMEM((2, width, tokens), bf16),
            pltpu.VMEM((np_, width, wide - lo), bf16),
            pltpu.VMEM(w_cross.shape, bf16),
            pltpu.VMEM((2, width, wide), bf16),
            pltpu.SemaphoreType.DMA((4,)),
        ],
        (
            da2,
            x2,
            cot,
            z1,
            cq,
            ck,
            cv,
            c1,
            oc,
            text,
            rows,
            w_self,
            w_cross,
            grad.reshape(grid.ay, grid.ax, grid.nz, grid.nc, own_rows, wide),
        ),
        63,
        pl.CostEstimate(
            flops=11 * tokens * width * width, bytes_accessed=50 * MIB, transcendentals=0
        ),
    )


def last_kernel(
    grid,
    a1,
    grad_qkv,
    att_t,
    dz1,
    lat,
    dx1,
    words,
    rows_ref,
    sums,
    mlp_sums,
    du_sums,
    own_up,
    own_down,
    w_self,
    w_cross,
    column_ref,
    own_ref,
    tokens_ref,
    words_ref,
    time_ref,
    own_table,
    norm_ref,
    *refs,
):
    scratch, refs = refs[:4], refs[4:]
    slab, a1_t, by_dp, back_t, weights, table_all, table_in = refs[:7]
    column_own, column_got = refs[7:9]
    table_got, table_sum, table_dp, tile, tile_got, tile_sum, tile_dp, sems = refs[9:17]
    np_, width, wide = w_self.shape
    tokens = a1.shape[0]
    cw = wide // 4
    nc, rows = grid.nc, wide and slab.shape[4]
    lo, hi = cw // 128 * 128, min(wide, -(-3 * cw // 128) * 128)
    loads = [
        pltpu.make_async_copy(w_self.at[p], weights.at[p % 2], sems.at[p % 2]) for p in range(np_)
    ] + [
        pltpu.make_async_copy(
            w_cross.at[p, :, pl.ds(lo, hi - lo)],
            weights.at[(np_ + p) % 2, :, pl.ds(0, hi - lo)],
            sems.at[(np_ + p) % 2],
        )
        for p in range(np_)
    ]
    loads[0].start()
    loads[1].start()

    def weight(k):
        loads[k].wait()
        return weights.at[k % 2]

    def used(k):
        if k + 2 < len(loads):
            loads[k + 2].start()

    site = Site(grid, *refs[17:])
    flow = NearScatterFlow(site, slab, own_ref.at[0], None, *scratch)
    column_sum = ColumnSum(site, column_ref, own_ref.at[1], column_own, column_got)
    column_sum.start()
    flat = flip(a1[...]).astype(bf16)
    span = nc * rows
    for z in range(grid.nz):
        a1_t[z] = flat[z * span : (z + 1) * span]
    heads = grad_qkv.shape[1]
    per_block = cw // HEAD_DIM
    for p in range(np_):
        for h in range(per_block):
            source, head = divmod(p * per_block + h, heads)
            for j in range(3):
                at = j * cw + h * HEAD_DIM
                by_dp[p, at : at + HEAD_DIM] = grad_qkv[source, head, j]

    for n in range(grid.nz):
        zone = flow.zone(n)
        for p in range(np_):
            part = dot(a1_t[zone], by_dp[p], "nt").astype(bf16)
            rest = dot(att_t[zone], dz1[p]).astype(bf16)
            for c in range(nc):
                at = slice(c * rows, (c + 1) * rows)
                slab[n, c, p // grid.ax, p % grid.ax, :, 0 : 3 * cw] = part[at]
                slab[n, c, p // grid.ax, p % grid.ax, :, 3 * cw :] = rest[at]
        flow.load(n)
        if n == 1:
            flow.first(0)
    steps = sequence(flow.blocks())[1:]

    def advance(count):
        run(steps[:count])
        del steps[:count]

    advance(2)
    for p in range(np_):
        part = dot(weight(p)[:, 0 : 3 * cw], by_dp[p])
        back_t[...] = part if p == 0 else back_t[...] + part
        used(p)
        if np_ < 8 or p % 4 == 0:
            advance(1)
    grad = jnp.transpose(back_t[...])
    normed, rate = norm_parts(lat[...].astype(f32))
    tokens_ref[...] = dx1[...] + norm_back(grad, normed, rate, 1.0 + column(rows_ref, 0))
    for at, source, n in (
        (2, sums, 5),
        (3, sums, 0),
        (4, sums, 1),
        (5, mlp_sums, 1),
        (8, sums, 6),
        (9, sums, 3),
        (10, sums, 4),
        (11, sums, 2),
        (12, mlp_sums, 0),
    ):
        table_all[at : at + 1, :] = source[n : n + 1, :]
    for p in range(np_):
        at, lane = 13 + p * wide // width, p * wide % width
        table_all[at : at + 1, lane : lane + wide] = du_sums[p]
    table_all[0:1, :] = jnp.sum(grad, axis=0, keepdims=True)
    table_all[1:2, :] = jnp.sum(grad * normed, axis=0, keepdims=True)
    ones = jnp.ones((8, tokens), bf16)
    for p in range(np_):
        whole = dot(ones, by_dp[p], "nt")
        at = slice(p * cw, (p + 1) * cw)
        table_all[6:7, at] = whole[0:1, 0:cw]
        table_all[7:8, at] = whole[0:1, 2 * cw : 3 * cw]
    part = width // grid.ns
    for n in range(grid.ns):
        table_in[n] = table_all[0 : table_in.shape[1], n * part : (n + 1) * part]
    table = ExchangeFlow(site, table_in, table_got)
    table.start()
    advance(2)
    found = None
    for p in range(np_):
        w = weight(np_ + p)
        at = slice(p * cw, (p + 1) * cw)
        both = dot(words[:, at], w[:, cw - lo : 2 * cw - lo], "nt")
        at = slice(width + p * cw, width + (p + 1) * cw)
        both = both + dot(words[:, at], w[:, 2 * cw - lo : 3 * cw - lo], "nt")
        found = both if found is None else found + both
        used(np_ + p)
    words_ref[...] = found[0 : words_ref.shape[0]]
    table.finish()
    total = table_got[0]
    for n in range(1, grid.ns):
        total = total + table_got[n]
    table_sum[...] = total
    whole = SpreadFlow(site, table_sum, time_ref)
    whole.start()
    over = SpreadFlow(site, table_sum, table_dp, over_dp=True)
    over.start()
    advance(max(0, len(steps) - 2))
    over.finish()
    total = table_dp[0]
    for n in range(1, grid.np):
        total = total + table_dp[n]
    own_table[...] = total
    column_sum.finish()
    square = jnp.sum(own_ref[1] * own_ref[1], keepdims=True)
    for done in (own_up, own_down):
        square = square + jnp.sum(done[0] * done[0], keepdims=True)
    square = square + jnp.where(site.p == 0, 1.0, 0.0) * jnp.sum(total * total, keepdims=True)
    advance(2)
    flow.finish()
    square = square + jnp.sum(own_ref[0] * own_ref[0], keepdims=True)
    tile[...] = jnp.broadcast_to(square, tile.shape)
    near = SpreadFlow(site, tile, tile_got)
    near.start()
    near.finish()
    total = tile_got[0]
    for n in range(1, grid.ns):
        total = total + tile_got[n]
    tile_sum[...] = total
    far = SpreadFlow(site, tile_sum, tile_dp, over_dp=True)
    far.start()
    far.finish()
    total = tile_dp[0]
    for n in range(1, grid.np):
        total = total + tile_dp[n]
    norm_ref[...] = total
    whole.finish()
    site.copies.finish()


def last_sums(grid, a1, grad_qkv, att_t, dz1, lat, dx1, words, text_count, rows_in, sums, owns, w_self, w_cross, column, table_rows):
    np_, width, wide = w_self.shape
    rows, cols = column.shape[1:]
    tokens = a1.shape[0]
    small = (table_rows, width // grid.ns)
    tile = (8, 128)
    return move(
        grid,
        last_kernel,
        "last_sums",
        scatter_slots(grid) + grid.nz + 3 * grid.ns + 2 * grid.np,
        6,
        3,
        [
            jax.ShapeDtypeStruct((2, rows, cols), f32),
            jax.ShapeDtypeStruct((tokens, width), f32),
            jax.ShapeDtypeStruct((text_count, width), f32),
            jax.ShapeDtypeStruct((grid.ns,) + small, f32),
            jax.ShapeDtypeStruct(small, f32),
            jax.ShapeDtypeStruct(tile, f32),
        ],
        [VMEM, VMEM, VMEM, HBM, VMEM, VMEM],
        [VMEM] * 13 + [HBM] * 3,
        scatter_scratch(grid, rows, cols, mine=False)
        + [
            pltpu.VMEM((grid.nz, grid.nc, grid.ay, grid.ax, rows, cols), bf16),
            pltpu.VMEM((grid.nz, grid.nc * rows, tokens), bf16),
            pltpu.VMEM((np_, 3 * (wide // 4), tokens), bf16),
            pltpu.VMEM((width, tokens), f32),
            pltpu.VMEM((2, width, wide), bf16),
            pltpu.VMEM((-(-table_rows // 8) * 8, width), f32),
            pltpu.VMEM((grid.ns,) + small, f32),
            pltpu.VMEM((rows, cols), bf16),
            pltpu.VMEM((max(1, grid.nz - 1), rows, cols), bf16),
            pltpu.VMEM((grid.ns,) + small, f32),
            pltpu.VMEM(small, f32),
            pltpu.VMEM((grid.np,) + small, f32),
            pltpu.VMEM(tile, f32),
            pltpu.VMEM((grid.ns,) + tile, f32),
            pltpu.VMEM(tile, f32),
            pltpu.VMEM((grid.np,) + tile, f32),
            pltpu.SemaphoreType.DMA((2,)),
        ],
        (
            a1,
            grad_qkv,
            att_t.reshape(grid.nz, grid.nc * rows, tokens),
            dz1,
            lat,
            dx1,
            words,
            rows_in,
            *sums,
            *owns,
            w_self,
            w_cross,
            column,
        ),
        60,
    )


def layer_norm(tokens_in):
    center = tokens_in - jnp.mean(tokens_in, axis=-1, keepdims=True)
    spread = jnp.mean(center * center, axis=-1, keepdims=True)
    return center * lax.rsqrt(spread + norm_eps)


def modulate(tokens_in, shift_row, scale_row):
    return layer_norm(tokens_in) * (1.0 + scale_row) + shift_row


def adam_step(weight, gradient, first_moment, second_moment, factor):
    clipped = gradient * factor
    first_new = first_decay * first_moment + (1.0 - first_decay) * clipped
    second_new = second_decay * second_moment + (1.0 - second_decay) * clipped * clipped
    first_hat = first_new / (1.0 - first_decay**STEP)
    second_hat = second_new / (1.0 - second_decay**STEP)
    updated = weight - learn_rate * (
        first_hat / (jnp.sqrt(second_hat) + adam_eps) + weight_decay * weight
    )
    return (updated, first_new, second_new)


def body(
    grid,
    latents,
    time_embed,
    text_tokens,
    cotangent,
    w_attn,
    w_mlp,
    bias_table,
    attn_first,
    attn_second,
    mlp_first,
    mlp_second,
    table_first,
    table_second,
):
    np_, ns = grid.np, grid.ns
    tokens_in = latents[0].astype(f32)
    rows, width = tokens_in.shape
    text_rows = text_tokens[0]
    text_count = text_rows.shape[0]
    heads = width // HEAD_DIM
    per_block = heads // np_
    local_heads = heads // ns
    scale = HEAD_DIM ** (-0.5)
    own_rows, own_cols = w_attn.shape[1], w_attn.shape[2]
    wide = 4 * own_cols

    def pack(matrices):
        return matrices.reshape(2, 4, own_rows, own_cols).transpose(0, 2, 1, 3).reshape(2, own_rows, wide)

    def unpack(slab):
        return slab.reshape(2, own_rows, 4, own_cols).transpose(0, 2, 1, 3).reshape(8, own_rows, own_cols)

    attn_low = pack(w_attn.astype(bf16))
    mlp_low = w_mlp.astype(bf16)
    own = (attn_low[0], attn_low[1], mlp_low[0], mlp_low[1])
    forward = attention(
        grid, scale, own, bias_table.astype(bf16), time_embed[0], latents[0], text_rows
    )
    w_self, w_cross, w_up, w_down = [w.reshape(np_, width, wide) for w in forward[:4]]
    attended_t, qkv, mixed_wide, logs, act_in, biases = forward[4:10]
    z1, x2, c1, cq, text_k, text_v, cross_out, a2 = forward[10:]
    modulation = biases[0:6] + time_embed[0].astype(f32)
    attended_t = attended_t.reshape(width, rows)

    block_out, da2, grad_up, grad_down, du_sums, mlp_sums = mlp(
        a2,
        cotangent[0],
        x2,
        w_up,
        w_down,
        biases[13:17].reshape(np_, 1, wide),
        jnp.stack([modulation[5], biases[12]]),
    )
    text_share = -(-text_count // (8 * ns)) * 8
    grad_first, grad_attended, dz1, text_part, sums, own_up, grad_cross = cross_backward(
        grid,
        scale,
        da2,
        x2,
        cotangent[0],
        z1,
        cq,
        text_k,
        text_v,
        c1,
        cross_out,
        text_rows,
        jnp.stack([modulation[4], modulation[2]]),
        w_self,
        w_cross,
        grad_up,
        ns * text_share,
        own_rows,
    )
    own_down, grad_column, grad_qkv, text_sum = attention_back(
        grid,
        scale,
        (grad_down, grad_cross),
        grad_attended.reshape(ns, local_heads, HEAD_DIM, rows),
        text_part.reshape(ns, text_share, 2 * width),
        qkv,
        mixed_wide,
        logs,
        own_rows,
        wide,
    )
    table_rows = bias_table.shape[0]
    own_mlp = jnp.concatenate([own_up, own_down], axis=0)
    own_attn, grad_tokens, grad_words, time_table, own_table, squares = last_sums(
        grid,
        act_in,
        grad_qkv,
        attended_t,
        dz1,
        latents[0],
        grad_first,
        text_sum.reshape(ns * text_share, 2 * width),
        text_count,
        modulation[1:2],
        (sums, mlp_sums, du_sums),
        (own_up, own_down),
        w_self,
        w_cross,
        grad_column,
        table_rows,
    )
    grad_time = time_table[:, :6].transpose(1, 0, 2).reshape(6, width)
    own_attn = unpack(own_attn)
    square_total = squares[0, 0]
    grad_norm = jnp.sqrt(square_total)
    factor = jnp.minimum(1.0, clip_norm / (grad_norm + 1e-06))
    attn_new, attn_first_new, attn_second_new = adam_step(
        w_attn, own_attn, attn_first, attn_second, factor
    )
    mlp_new, mlp_first_new, mlp_second_new = adam_step(
        w_mlp, own_mlp, mlp_first, mlp_second, factor
    )
    table_new, table_first_new, table_second_new = adam_step(
        bias_table, own_table, table_first, table_second, factor
    )
    return (
        block_out[None],
        grad_tokens[None],
        grad_time[None],
        grad_words[None],
        grad_norm,
        attn_new,
        attn_new.astype(bf16),
        attn_first_new,
        attn_second_new,
        mlp_new,
        mlp_new.astype(bf16),
        mlp_first_new,
        mlp_second_new,
        table_new,
        table_new.astype(bf16),
        table_first_new,
        table_second_new,
        own_table[12],
    )


def solution(mesh):
    return jax.shard_map(
        functools.partial(body, Grid(mesh)),
        mesh=mesh,
        in_specs=(
            P("dp", "seq", None),
            P("dp", None, None),
            P("dp", None, None),
            P("dp", "seq", None),
            P(None, "seq", "dp"),
            P(None, "seq", "dp"),
            P(None, "seq"),
            P(None, "seq", "dp"),
            P(None, "seq", "dp"),
            P(None, "seq", "dp"),
            P(None, "seq", "dp"),
            P(None, "seq"),
            P(None, "seq"),
        ),
        out_specs=(
            P("dp", "seq", None),
            P("dp", "seq", None),
            P("dp", None, None),
            P("dp", None, None),
            P(),
            P(None, "seq", "dp"),
            P(None, "seq", "dp"),
            P(None, "seq", "dp"),
            P(None, "seq", "dp"),
            P(None, "seq", "dp"),
            P(None, "seq", "dp"),
            P(None, "seq", "dp"),
            P(None, "seq", "dp"),
            P(None, "seq"),
            P(None, "seq"),
            P(None, "seq"),
            P(None, "seq"),
            P("seq"),
        ),
        check_vma=False,
    )
```

```python
import functools
import math

import jax
import jax.numpy as jnp
from jax import lax
from jax.experimental import pallas as pl
from jax.experimental.pallas import tpu as pltpu
from jax.sharding import PartitionSpec as P

STEP = 10

norm_eps = 1e-06
clip_norm = 1.0
learn_rate = 0.02
first_decay = 0.5
second_decay = 0.5
adam_eps = 1e-08
weight_decay = 0.01

HEAD_DIM = 72
MESH = pl.DeviceIdType.MESH
f32 = jnp.float32
bf16 = jnp.bfloat16
MIB = 1 << 20


class Grid:
    def __init__(self, mesh):
        self.np = mesh.shape["dp"]
        self.ns = mesh.shape["seq"]
        root = math.isqrt(self.np)
        self.ax = root if root * root == self.np else self.np
        self.ay = self.np // self.ax
        self.nc = 2 if self.ns % 2 == 0 else 1
        self.nz = self.ns // self.nc
        self.paired = self.nz & (self.nz - 1) == 0

    def here(self):
        p = lax.axis_index("dp")
        s = lax.axis_index("seq")
        return p // self.ax, p % self.ax, s // self.nc, s % self.nc

    def device(self, y, x, z, c):
        return (y * self.ax + x, z * self.nc + c)


def turn(value, step, size):
    return (value + step) % size


class Copies:
    def __init__(self, send_sem, recv_sem, me):
        self.send_sem, self.recv_sem, self.me = send_sem, recv_sem, me
        self.started = []
        self.count = 0

    def make(self, slot, into, src, dst, device):
        return pltpu.make_async_remote_copy(
            src_ref=src,
            dst_ref=dst,
            send_sem=self.send_sem.at[slot],
            recv_sem=self.recv_sem.at[into],
            device_id=device,
            device_id_type=MESH,
        )

    def reserve(self):
        self.count += 1
        return self.count - 1

    def send(self, refs, into=None, when=None):
        slot = self.reserve()
        into = slot if into is None else into
        self.started.append((slot, into, refs, when))

        def start():
            self.make(slot, into, *refs()).start()

        if when is None:
            start()
        else:
            pl.when(when())(start)
        return slot

    def arrived(self, slot, landed):
        self.make(slot, slot, landed, landed, self.me).wait_recv()

    def finish(self):
        for slot, into, refs, when in self.started:

            def done(slot=slot, into=into, refs=refs):
                self.make(slot, into, *refs()).wait_send()

            if when is None:
                done()
            else:
                pl.when(when())(done)


class Local:
    def __init__(self, sems, slot, refs):
        self.sems, self.slot, self.refs = sems, slot, refs
        pltpu.make_async_copy(*refs(), sems.at[slot]).start()

    def wait(self):
        pltpu.make_async_copy(*self.refs(), self.sems.at[self.slot]).wait()


def greet(devices):
    barrier = pltpu.get_barrier_semaphore()
    for device in devices:
        pl.semaphore_signal(barrier, inc=1, device_id=device, device_id_type=MESH)
    pl.semaphore_wait(barrier, len(devices))


def partners(grid, y, x, z, c):
    p, s = grid.device(y, x, z, c)
    found = [(p, turn(s, r, grid.ns)) for r in range(1, grid.ns)]
    found += [(turn(p, r, grid.np), s) for r in range(1, grid.np)]
    return found


def flip_bits(value, r):
    out, bit = value, 1
    while bit <= r:
        if r & bit:
            out = out + bit * (1 - 2 * ((value // bit) % 2))
        bit *= 2
    return out


class Site:
    def __init__(self, grid, send_sem, recv_sem, local_sem):
        self.grid = grid
        self.y, self.x, self.z, self.c = grid.here()
        self.p, self.s = grid.device(self.y, self.x, self.z, self.c)
        self.copies = Copies(send_sem, recv_sem, (self.p, self.s))
        self.local_sem = local_sem
        self.locals = 0
        greet(partners(grid, self.y, self.x, self.z, self.c))

    def local(self, refs):
        self.locals += 1
        return Local(self.local_sem, self.locals - 1, refs)

    def along(self, first_x, r, second=False):
        g = self.grid
        if first_x != second:
            return g.device(self.y, turn(self.x, r, g.ax), self.z, self.c)
        return g.device(turn(self.y, r, g.ay), self.x, self.z, self.c)

    def z_to(self, r):
        return flip_bits(self.z, r) if self.grid.paired else turn(self.z, r, self.grid.nz)

    def z_from(self, r):
        return flip_bits(self.z, r) if self.grid.paired else turn(self.z, self.grid.nz - r, self.grid.nz)

    def z_device(self, r):
        return self.grid.device(self.y, self.x, self.z_to(r), self.c)

    def other_core(self):
        return self.grid.device(self.y, self.x, self.z, 1 - self.c)


def pieces_of(rows, i):
    cut = (rows // 2 + 15) // 16 * 16
    if rows % 16 == 0 and cut < rows:
        return [(0, cut, True), (cut, rows - cut, False)]
    return [(0, rows, i % 2 == 0)]


def sequence(blocks, lead=1):
    steps = []
    for i in range(len(blocks) + 2):
        for ahead in range(lead + 1) if i == 0 else (lead,):
            if i + ahead < len(blocks):
                flow, n = blocks[i + ahead]
                steps.append(("F", i + ahead, functools.partial(flow.first, n)))
        if i < len(blocks):
            flow, n = blocks[i]
            steps.append(("S", i, functools.partial(flow.second, n)))
        if 0 <= i - 1 < len(blocks):
            flow, n = blocks[i - 1]
            steps.append(("T", i - 1, functools.partial(flow.third, n)))
    return steps


def run(steps):
    for _, _, step in steps:
        step()


class ZPhase:
    def __init__(self, site, own_ref, landing):
        self.site, self.own, self.landing = site, own_ref, landing
        self.relay = site.grid.nz == 4
        self.slots = {}

    def inner(self):
        z = self.site.z
        return z * (3 - z) // 2

    def place(self, k):
        t = self.site
        if k == 0:
            return t.z
        if not self.relay:
            return t.z_from(k)
        if k == 1:
            return flip_bits(t.z, 1)
        near = self.inner() if k == 2 else 1 - self.inner()
        return near * (3 - t.z) + (1 - near) * flip_bits(t.z, 2)

    def block(self, k):
        return self.landing(self.place(k))

    def start(self):
        t = self.site
        if not self.relay:
            for k in range(1, t.grid.nz):
                self.slots[k] = t.copies.send(
                    lambda k=k: (self.own, self.landing(t.z), t.z_device(k))
                )
            return
        self.slots[1] = t.copies.send(
            lambda: (self.own, self.landing(t.z), t.z_device(1))
        )
        self.slots[2] = t.copies.reserve()
        self.slots[3] = t.copies.reserve()
        t.copies.send(
            lambda: (self.own, self.landing(t.z), t.z_device(3)),
            self.slots[2],
            lambda: self.inner() == 1,
        )

    def pass_on(self, k):
        if not self.relay:
            return
        t = self.site
        pl.when(self.inner() == 1)(lambda: t.copies.arrived(self.slots[k], self.block(k)))
        t.copies.send(
            lambda: (self.block(k), self.block(k), t.z_device(3 if k == 1 else 1)),
            self.slots[3 if k == 1 else k],
            lambda: self.inner() == 1,
        )

    def settle(self, k):
        def wait():
            self.site.copies.arrived(self.slots[k], self.block(k))

        if self.relay:
            pl.when(self.inner() == 0)(wait)
        else:
            wait()


class GatherFlow:
    def __init__(self, site, out_ref, own_ref):
        self.site, self.out, self.own = site, out_ref, own_ref
        self.rows = out_ref.shape[4]
        self.count = site.grid.nz
        self.zone = ZPhase(site, own_ref, lambda z: self.out.at[site.y, site.x, z, site.c])
        self.slots = {}

    def mine(self, n, piece=None):
        t = self.site
        if piece is None:
            return self.out.at[t.y, t.x, self.zone.place(n), t.c]
        return self.out.at[t.y, t.x, self.zone.place(n), t.c, pl.ds(piece[0], piece[1])]

    def spot(self, n, piece, dy, dx):
        t, g = self.site, self.site.grid
        return self.out.at[
            turn(t.y, g.ay - dy, g.ay),
            turn(t.x, g.ax - dx, g.ax),
            self.zone.place(n),
            t.c,
            pl.ds(piece[0], piece[1]),
        ]

    def plane(self, n, c):
        return self.out.at[:, :, self.zone.place(n), c]

    def start(self):
        self.local = self.site.local(lambda: (self.own, self.mine(0)))

    def first(self, n):
        t, g = self.site, self.site.grid
        if n:
            self.zone.settle(n)

        def refs(piece, first_x, step):
            source = self.own.at[pl.ds(piece[0], piece[1])] if n == 0 else self.mine(n, piece)
            return source, self.mine(n, piece), t.along(first_x, step)

        for piece in pieces_of(self.rows, n):
            for first_x in (piece[2], not piece[2]):
                for step in range(1, g.ax if first_x else g.ay):
                    self.slots["a", n, piece, first_x, step] = t.copies.send(
                        functools.partial(refs, piece, first_x, step)
                    )

    def second(self, n):
        t, g = self.site, self.site.grid
        for piece in pieces_of(self.rows, n):
            first_x = piece[2]
            for step in range(1, g.ax if first_x else g.ay):
                dy, dx = (0, step) if first_x else (step, 0)
                t.copies.arrived(
                    self.slots["a", n, piece, first_x, step], self.spot(n, piece, dy, dx)
                )

                def refs(piece, dy, dx, onward):
                    block = self.spot(n, piece, dy, dx)
                    return block, block, t.along(piece[2], onward, True)

                for onward in range(1, g.ay if first_x else g.ax):
                    self.slots["b", n, piece, step, onward] = t.copies.send(
                        functools.partial(refs, piece, dy, dx, onward)
                    )

    def third(self, n):
        t, g = self.site, self.site.grid
        for piece in pieces_of(self.rows, n):
            first_x = piece[2]
            for onward in range(1, g.ay if first_x else g.ax):
                dy, dx = (onward, 0) if first_x else (0, onward)
                t.copies.arrived(
                    self.slots["a", n, piece, not first_x, onward], self.spot(n, piece, dy, dx)
                )
                for step in range(1, g.ax if first_x else g.ay):
                    dy, dx = (onward, step) if first_x else (step, onward)
                    t.copies.arrived(
                        self.slots["b", n, piece, step, onward], self.spot(n, piece, dy, dx)
                    )
        if n == 0:
            self.local.wait()
        if g.nc > 1:
            self.slots["c", n] = t.copies.send(
                lambda: (self.plane(n, t.c), self.plane(n, t.c), t.other_core())
            )

    def blocks(self):
        return [(self, n) for n in range(self.count)]

    def relays(self):
        return [
            ("P", k, functools.partial(self.zone.pass_on, k)) for k in range(1, self.count)
        ]

    def finish(self):
        t, g = self.site, self.site.grid
        if g.nc > 1:
            for n in range(self.count):
                t.copies.arrived(self.slots["c", n], self.plane(n, 1 - t.c))


def weave(steps, extra):
    found = []
    for step in steps:
        found.append(step)
        found += extra.get(step[:2], [])
    return found


def add_rows(dst, srcs, lo, count):
    chunk = max([n for n in range(16, 49, 16) if count % n == 0], default=count)
    for j in range(count // chunk):
        at = pl.ds(lo + j * chunk, chunk)
        if len(srcs) == 2 and dst.dtype == bf16:
            dst[at] = srcs[0][at] + srcs[1][at]
            continue
        total = srcs[0][at].astype(f32)
        for src in srcs[1:]:
            total = total + src[at].astype(f32)
        dst[at] = total.astype(dst.dtype)


def add_blocks(count, pick, lo, rows):
    def body(i, carry):
        dst, srcs = pick(i)
        add_rows(dst, srcs, lo, rows)
        return carry

    lax.fori_loop(0, count, body, 0)


class ScatterFlow:
    def __init__(self, site, grad_ref, out_ref, mine, half_sum, got_a, got_b, got_z, column_ref=None):
        self.site, self.grad, self.out, self.column = site, grad_ref, out_ref, column_ref
        self.mine, self.half_sum, self.got_a, self.got_b, self.got_z = mine, half_sum, got_a, got_b, got_z
        self.order = list(range(site.grid.nz))[::-1]
        self.slots = {}
        self.locals = {}
        self.base = 0
        self.then = {}
        self.rows = half_sum.shape[3]

    def zone(self, n):
        r = self.order[n]
        return self.site.z_to(r) if r else self.site.z

    def load(self, n):
        t, g = self.site, self.site.grid
        if g.nc > 1:
            self.slots["core", n] = t.copies.send(
                lambda: (
                    self.grad.at[:, :, self.zone(n), 1 - t.c],
                    self.half_sum.at[n],
                    t.other_core(),
                )
            )
        self.locals[n] = t.local(
            lambda: (self.grad.at[:, :, self.zone(n), t.c], self.mine.at[self.spot(n)])
        )

    def own_part(self, n, a, b):
        return self.mine.at[self.spot(n), a, b]

    def spot(self, n):
        return (self.base + n) % self.mine.shape[0]

    def first(self, n):
        t, g = self.site, self.site.grid
        if n in self.locals:
            self.locals[n].wait()
        if g.nc > 1:
            t.copies.arrived(self.slots["core", n], self.half_sum.at[n])

        def pick(i):
            dst = self.half_sum.at[n, i // g.ax, i % g.ax]
            return dst, [self.own_part(n, i // g.ax, i % g.ax)] + ([dst] if g.nc > 1 else [])

        add_blocks(g.ay * g.ax, pick, 0, self.rows)
        if n in self.then:
            self.then[n]()

        def refs(piece, step):
            at = pl.ds(piece[0], piece[1])
            if piece[2]:
                source = self.half_sum.at[n, :, turn(t.x, step, g.ax), at]
            else:
                source = self.half_sum.at[n, turn(t.y, step, g.ay), :, at]
            return source, self.landing(n, piece, step), t.along(piece[2], step)

        for piece in pieces_of(self.rows, n):
            for step in range(1, g.ax if piece[2] else g.ay):
                self.slots["a", n, piece, step] = t.copies.send(
                    functools.partial(refs, piece, step)
                )

    def landing(self, n, piece, step):
        g = self.site.grid
        return self.got_a.at[
            n, step - 1, pl.ds(0, g.ay if piece[2] else g.ax), pl.ds(piece[0], piece[1])
        ]

    def second(self, n):
        t, g = self.site, self.site.grid
        for piece in pieces_of(self.rows, n):
            lo, rows, first_x = piece
            at = pl.ds(lo, rows)
            count, across = (g.ax, g.ay) if first_x else (g.ay, g.ax)
            for step in range(1, count):
                t.copies.arrived(self.slots["a", n, piece, step], self.landing(n, piece, step))

            def pick(i):
                dst = self.half_sum.at[n, i, t.x] if first_x else self.half_sum.at[n, t.y, i]
                return dst, [dst] + [self.got_a.at[n, step - 1, i] for step in range(1, count)]

            add_blocks(across, pick, lo, rows)

            def refs(step, first_x=first_x, at=at):
                if first_x:
                    source = self.half_sum.at[n, turn(t.y, step, g.ay), t.x, at]
                else:
                    source = self.half_sum.at[n, t.y, turn(t.x, step, g.ax), at]
                return source, self.got_b.at[n, step - 1, at], t.along(first_x, step, True)

            for step in range(1, across):
                self.slots["b", n, piece, step] = t.copies.send(functools.partial(refs, step))

    def third(self, n):
        t, g = self.site, self.site.grid
        r = self.order[n]
        own = self.half_sum.at[n, t.y, t.x]
        into = own if self.column is None else self.column.at[r]
        for piece in pieces_of(self.rows, n):
            lo, rows, first_x = piece
            across = g.ay if first_x else g.ax
            for step in range(1, across):
                t.copies.arrived(
                    self.slots["b", n, piece, step], self.got_b.at[n, step - 1, pl.ds(lo, rows)]
                )
            add_rows(into, [own] + [self.got_b.at[n, step - 1] for step in range(1, across)], lo, rows)
        if self.column is None and r:
            self.slots["z", r] = t.copies.send(
                lambda: (self.half_sum.at[n, t.y, t.x], self.got_z.at[r - 1], t.z_device(r))
            )

    def blocks(self):
        return [(self, n) for n in range(len(self.order))]

    def finish(self):
        if self.column is not None:
            return
        t, g = self.site, self.site.grid
        for r in range(1, g.nz):
            t.copies.arrived(self.slots["z", r], self.got_z.at[r - 1])
        own = self.half_sum.at[len(self.order) - 1, t.y, t.x]
        add_rows(
            self.out, [own] + [self.got_z.at[r - 1] for r in range(1, g.nz)], 0, self.rows
        )


class NearScatterFlow(ScatterFlow):
    def load(self, n):
        t = self.site
        if t.grid.nc > 1:
            self.slots["core", n] = t.copies.send(
                lambda: (self.grad.at[n, 1 - t.c], self.half_sum.at[n], t.other_core())
            )

    def own_part(self, n, a, b):
        return self.grad.at[n, self.site.c, a, b]


class ColumnSum:
    def __init__(self, site, column_ref, out_ref, own, got_z):
        self.site, self.column, self.out, self.own, self.got_z = site, column_ref, out_ref, own, got_z
        self.rows = own.shape[0]

    def start(self):
        t = self.site
        self.local = t.local(lambda: (self.column.at[0], self.own))
        self.slots = {
            r: t.copies.send(
                lambda r=r: (self.column.at[r], self.got_z.at[r - 1], t.z_device(r))
            )
            for r in range(1, t.grid.nz)
        }

    def finish(self):
        t = self.site
        self.local.wait()
        for r, slot in self.slots.items():
            t.copies.arrived(slot, self.got_z.at[r - 1])
        add_rows(
            self.out,
            [self.own] + [self.got_z.at[r - 1] for r in range(1, t.grid.nz)],
            0,
            self.rows,
        )


def load_in_turn(blocks):
    depth = blocks[0][0].mine.shape[0]
    for i, (flow, n) in enumerate(blocks):
        if n == 0:
            flow.base = i
    for i, (flow, n) in enumerate(blocks):
        if i < depth:
            flow.load(n)
        if i + depth < len(blocks):
            later, m = blocks[i + depth]
            flow.then[n] = functools.partial(later.load, m)


def scatter_scratch(grid, rows, cols, mine=True):
    block = (rows, cols)
    widest = max(grid.ax, grid.ay)
    depth = min(grid.nz, 2)
    found = [pltpu.VMEM((depth, grid.ay, grid.ax) + block, bf16)] if mine else []
    return found + [
        pltpu.VMEM((grid.nz, grid.ay, grid.ax) + block, bf16),
        pltpu.VMEM((grid.nz, max(1, widest - 1), widest) + block, bf16),
        pltpu.VMEM((grid.nz, max(1, widest - 1)) + block, bf16),
        pltpu.VMEM((max(1, grid.nz - 1),) + block, bf16),
    ]


def by_distance(size):
    return sorted(range(1, size), key=lambda r: (min(r, size - r), r))


class ExchangeFlow:
    def __init__(self, site, in_ref, out_ref, head=None, part=None):
        self.site, self.src, self.dst = site, in_ref, out_ref
        self.index = () if head is None else (head,) if part is None else (head, part)
        self.slots = {}

    def at(self, ref, n):
        return ref.at[(n,) + self.index]

    def start_one(self, r):
        t, ns = self.site, self.site.grid.ns
        if r == 0:
            self.own = t.local(lambda: (self.at(self.src, t.s), self.at(self.dst, t.s)))
            return
        self.slots[r] = t.copies.send(
            lambda: (
                self.at(self.src, turn(t.s, r, ns)),
                self.at(self.dst, t.s),
                (t.p, turn(t.s, r, ns)),
            )
        )

    def start(self):
        for r in by_distance(self.site.grid.ns)[::-1] + [0]:
            self.start_one(r)

    def finish(self):
        t, ns = self.site, self.site.grid.ns
        self.own.wait()
        for r, slot in self.slots.items():
            t.copies.arrived(slot, self.at(self.dst, turn(t.s, ns - r, ns)))


class SpreadFlow:
    def __init__(self, site, in_ref, out_ref, over_dp=False):
        self.site, self.src, self.dst, self.over_dp = site, in_ref, out_ref, over_dp
        g = site.grid
        self.size, self.place = (g.np, site.p) if over_dp else (g.ns, site.s)

    def start(self):
        t = self.site

        def refs(r):
            to = turn(self.place, r, self.size)
            return self.src, self.dst.at[self.place], (to, t.s) if self.over_dp else (t.p, to)

        self.slots = {
            r: t.copies.send(functools.partial(refs, r)) for r in by_distance(self.size)
        }
        self.own = t.local(lambda: (self.src, self.dst.at[self.place]))

    def finish(self):
        self.own.wait()
        for r, slot in self.slots.items():
            self.site.copies.arrived(slot, self.dst.at[turn(self.place, self.size - r, self.size)])


def flip(block):
    return jnp.transpose(block.astype(f32))


def attend_head(qkv, head, keys, values):
    sources, rows = qkv.shape[0], qkv.shape[-1]
    for s in range(sources):
        at = slice(s * rows, (s + 1) * rows)
        keys[:, at] = qkv[s, head, 1]
        values[at, :] = flip(qkv[s, head, 2]).astype(bf16)


def attend_block(scale, qkv, head, block, out, wide, logs, keys, values, scores):
    sources, rows = qkv.shape[0], qkv.shape[-1]
    query = flip(qkv[block, head, 0]).astype(bf16)
    factor = scale * math.log2(math.e)
    peak = None
    for s in range(sources):
        at = slice(s * rows, (s + 1) * rows)
        part = jnp.dot(query, keys[:, at], preferred_element_type=f32)
        scores[:, at] = part
        top = jnp.max(part, axis=-1, keepdims=True)
        peak = top if peak is None else jnp.maximum(peak, top)
    peak = peak * factor
    total = jnp.zeros((rows, 1), f32)
    mixed = jnp.zeros((rows, HEAD_DIM), f32)
    for s in range(sources):
        at = slice(s * rows, (s + 1) * rows)
        part = jnp.exp2(scores[:, at] * factor - peak)
        total = total + jnp.sum(part, axis=-1, keepdims=True)
        mixed = mixed + jnp.dot(part.astype(bf16), values[at, :], preferred_element_type=f32)
    mixed = jnp.transpose(mixed / total)
    wide[head, block] = mixed
    out[block, head] = mixed.astype(bf16)
    logs[head, block] = jnp.transpose(jnp.broadcast_to(peak + jnp.log2(total), (rows, 8)))


def attend_scratch(qkv):
    sources, _, _, dim, rows = qkv.shape
    length = sources * rows
    return [
        pltpu.VMEM((dim, length), bf16),
        pltpu.VMEM((length, dim), bf16),
        pltpu.VMEM((rows, length), f32),
    ]


def attend_back_head(qkv, head, keys, key_rows, values, grad_k, grad_v):
    sources, rows = qkv.shape[0], qkv.shape[-1]
    for s in range(sources):
        at = slice(s * rows, (s + 1) * rows)
        keys[:, at] = qkv[s, head, 1]
        key_rows[at, :] = flip(qkv[s, head, 1]).astype(bf16)
        values[:, at] = qkv[s, head, 2]
    grad_k[...] = jnp.zeros_like(grad_k)
    grad_v[...] = jnp.zeros_like(grad_v)


def attend_back_block(
    scale, qkv, grad_in, wide, logs, head, block, out, keys, key_rows, values, grad_k, grad_v
):
    sources, rows = qkv.shape[0], qkv.shape[-1]
    query_t = qkv[block, head, 0]
    grad_t = grad_in[block, head]
    query = flip(query_t).astype(bf16)
    grad = flip(grad_t).astype(bf16)
    factor = scale * math.log2(math.e)
    inner = jnp.sum(grad_t.astype(f32) * wide[head, block], axis=0, keepdims=True)
    inner = jnp.transpose(jnp.broadcast_to(inner, (8, rows)))[:, 0:1]
    log_rows = jnp.transpose(logs[head, block])[:, 0:1]
    grad_q = jnp.zeros((rows, HEAD_DIM), f32)
    for s in range(sources):
        at = slice(s * rows, (s + 1) * rows)
        part = jnp.dot(query, keys[:, at], preferred_element_type=f32)
        probs = jnp.exp2(part * factor - log_rows)
        grad_p = jnp.dot(grad, values[:, at], preferred_element_type=f32)
        grad_s = (probs * (grad_p - inner)).astype(bf16)
        grad_q = grad_q + jnp.dot(grad_s, key_rows[at, :], preferred_element_type=f32)
        grad_k[:, at] += jnp.dot(query_t, grad_s, preferred_element_type=f32)
        grad_v[:, at] += jnp.dot(grad_t, probs.astype(bf16), preferred_element_type=f32)
    out[block, head, 0] = jnp.transpose(grad_q * scale).astype(bf16)


def attend_back_end(scale, head, out, grad_k, grad_v):
    sources, rows = out.shape[0], out.shape[-1]
    for s in range(sources):
        at = slice(s * rows, (s + 1) * rows)
        out[s, head, 1] = (grad_k[:, at] * scale).astype(bf16)
        out[s, head, 2] = grad_v[:, at].astype(bf16)


def attend_back_scratch(qkv):
    sources, _, _, dim, rows = qkv.shape
    length = sources * rows
    return [
        pltpu.VMEM((dim, length), bf16),
        pltpu.VMEM((length, dim), bf16),
        pltpu.VMEM((dim, length), bf16),
        pltpu.VMEM((dim, length), f32),
        pltpu.VMEM((dim, length), f32),
    ]


VMEM = pl.BlockSpec(memory_space=pltpu.VMEM)
HBM = pl.BlockSpec(memory_space=pltpu.HBM)


def gather_shape(grid, rows, cols):
    return jax.ShapeDtypeStruct((grid.ay, grid.ax, grid.nz, grid.nc, rows, cols), bf16)


def gather_slots(grid):
    across = 2 * (grid.ax + grid.ay - 2) + 2 * (grid.ax - 1) * (grid.ay - 1)
    return grid.nz + 6 + grid.nz * (across + 1)


def scatter_slots(grid):
    return grid.nz * (2 * (grid.ax + grid.ay - 2) + 1) + grid.nz - 1


def move(grid, kernel, name, slots, locals_, call_id, out_shape, out_specs, in_specs, scratch, args, vmem, cost=None):
    return pl.pallas_call(
        functools.partial(kernel, grid),
        name=name,
        out_shape=out_shape,
        in_specs=in_specs,
        out_specs=out_specs,
        scratch_shapes=list(scratch)
        + [
            pltpu.SemaphoreType.DMA((slots,)),
            pltpu.SemaphoreType.DMA((slots,)),
            pltpu.SemaphoreType.DMA((locals_,)),
        ],
        compiler_params=pltpu.CompilerParams(
            collective_id=call_id, has_side_effects=True, vmem_limit_bytes=vmem * MIB
        ),
        cost_estimate=cost,
    )(*args)


def planned(steps, times, when):
    inside, rest = [], []
    at = 0
    for kind, n, step in steps:
        while at < len(times) and times[at] < when(kind, n):
            at += 1
        if at < len(times):
            inside.append((at, step))
        else:
            rest.append((kind, n, step))
    return inside, rest


def attention_kernel(
    grid,
    scale,
    own_0,
    own_a,
    own_b,
    own_c,
    table_ref,
    time_ref,
    lat,
    text,
    out_0,
    out_a,
    out_b,
    out_c,
    back_ref,
    qkv,
    wide,
    logs,
    a1,
    biases,
    z1,
    x2,
    c1,
    cq,
    ck,
    cv,
    oc,
    a2,
    *refs,
):
    mixed, keys, values, scores, table_all, parts, weights, att, sems = refs[:9]
    site = Site(grid, *refs[9:])
    heads, sources = qkv.shape[1], qkv.shape[0]
    tokens, width = a1.shape
    cols = weights.shape[4]
    cw = cols // 4
    rows = own_0.shape[0]
    nz, nc = grid.nz, grid.nc
    flows = [
        GatherFlow(site, out, own)
        for out, own in ((out_0, own_0), (out_a, own_a), (out_b, own_b), (out_c, own_c))
    ]
    incoming = [ExchangeFlow(site, parts, qkv, h) for h in range(heads)]
    outgoing = [ExchangeFlow(site, mixed, back_ref, h) for h in range(heads)]
    table = SpreadFlow(site, table_ref, table_all)
    table.start()
    flows[0].start()
    flows[0].zone.start()
    flows[0].first(0)
    for flow in flows[1:]:
        flow.start()
    relays = [flow.relays() for flow in flows]
    zones = [[("Z", k, flow.zone.start)] for k, flow in enumerate(flows)]
    steps = weave(
        sequence([block for flow in flows for block in flow.blocks()]),
        {
            ("F", 0): relays[0][:1],
            ("F", 1): relays[0][1:2],
            ("S", 0): relays[0][2:] + zones[1],
            ("S", 1): relays[1][:1],
            ("F", 3): relays[1][1:2],
            ("S", 2): relays[1][2:] + zones[2],
            ("S", 3): relays[2][:1],
            ("F", 5): relays[2][1:2],
            ("S", 4): relays[2][2:],
        },
    )[1:]

    normed, _ = norm_parts(lat[...].astype(f32))
    table.finish()
    part = table_ref.shape[1]
    for n in range(grid.ns):
        biases[:, n * part : (n + 1) * part] = table_all[n].astype(f32)
    shift = biases[0:1, :] + time_ref[0:1, :].astype(f32)
    gain = 1.0 + biases[1:2, :] + time_ref[1:2, :].astype(f32)
    a1[...] = (normed * gain + shift).astype(bf16)

    cut = max(i for i, (kind, n, _) in enumerate(steps) if kind == "T" and n == nz - 1) + 1
    run(steps[:cut])
    flows[0].finish()

    order = [(out, p) for out in (out_0, out_0, out_a, out_a) for p in range(grid.np)]

    def load(k):
        out, p = order[k]
        return pltpu.make_async_copy(
            out.at[p // grid.ax, p % grid.ax], weights.at[k % 2], sems.at[k % 2]
        )

    def through(left, k, lo, hi):
        slot = weights.at[k % 2]
        if rows % 16 == 0:
            return dot(left[...], slot[:, :, :, lo:hi].reshape(width, hi - lo))
        found = None
        for n in range(nz * nc):
            piece = dot(left[:, n * rows : (n + 1) * rows], slot[n // nc, n % nc, :, lo:hi])
            found = piece if found is None else found + piece
        return found

    def used(k):
        if k + 2 < len(order):
            load(k + 2).start()

    load(0).start()
    load(1).start()
    for p in range(grid.np):
        load(p).wait()
        found = through(a1, p, 0, 3 * cw)
        used(p)
        found = jnp.transpose(found)
        at = slice(p * cw, (p + 1) * cw)
        rows_q = jnp.transpose(jnp.broadcast_to(biases[6:7, at], (8, cw)))[:, 0:1]
        rows_v = jnp.transpose(jnp.broadcast_to(biases[7:8, at], (8, cw)))[:, 0:1]
        thirds = (found[0:cw] + rows_q, found[cw : 2 * cw], found[2 * cw : 3 * cw] + rows_v)
        for h in range(cw // HEAD_DIM):
            device, head = divmod(p * (cw // HEAD_DIM) + h, heads)
            for j in range(3):
                parts[device, head, j] = thirds[j][h * HEAD_DIM : (h + 1) * HEAD_DIM].astype(bf16)
    incoming[0].start()

    def due(kind, n):
        return 11.5 * n + {"F": -16, "S": 2, "T": 14, "P": 0, "Z": 0}[kind]

    cut_b = max([i + 1 for i, (kind, n, _) in enumerate(steps) if due(kind, n) <= 86] + [cut])
    run(steps[cut:cut_b])
    incoming[0].finish()
    for flow in incoming[1:2]:
        flow.start()
    times = [92 + 29 * (i // sources) + 2.4 * (i % sources) for i in range(heads * sources)]
    inside, rest = planned(steps[cut_b:], times, due)
    for n, (_, _, step) in enumerate(zones[3] + relays[3]):
        inside.append(((heads - 1) * sources + min(2 * n, sources - 1), step))

    def turn_of(i, carry):
        head, block = i // sources, turn(site.s, i, sources)
        for h in range(1, heads):

            @pl.when(i == h * sources)
            def _():
                incoming[h].finish()
                for flow in incoming[h + 1 : h + 2]:
                    flow.start()

        @pl.when(i % sources == 0)
        def _():
            attend_head(qkv, head, keys, values)

        attend_block(scale, qkv, head, block, mixed, wide, logs, keys, values, scores)
        for h in range(heads):
            for r in range(sources):
                pl.when(i == h * sources + r)(functools.partial(outgoing[h].start_one, r))
        for at in sorted({n for n, _ in inside}):

            @pl.when(i == at)
            def _():
                for n, step in inside:
                    if n == at:
                        step()

        return carry

    lax.fori_loop(0, heads * sources, turn_of, 0)

    def advance(count):
        run(rest[:count])
        del rest[:count]

    def vector(n):
        return biases[n : n + 1, :] + time_ref[n : n + 1, :].astype(f32)

    advance(max([i + 1 for i, (_, n, _) in enumerate(rest) if n < 2 * nz] + [0]))
    flows[1].finish()
    for flow in outgoing:
        flow.finish()
    for n in range(sources * heads):
        at = slice(n * HEAD_DIM, (n + 1) * HEAD_DIM)
        att[:, at] = flip(back_ref[n // heads, n % heads]).astype(bf16)
    k = grid.np
    for p in range(grid.np):
        at = slice(p * cw, (p + 1) * cw)
        load(k + p).wait()
        z1[:, at] = through(att, k + p, 3 * cw, 4 * cw) + biases[8:9, at]
        used(k + p)
    advance(2)
    x1 = lat[...].astype(f32) + vector(2) * z1[...]
    x2[...] = x1
    c1[...] = x1.astype(bf16)
    k += grid.np
    for p in range(grid.np):
        at = slice(p * cw, (p + 1) * cw)
        load(k + p).wait()
        ck[:, at] = through(text, k + p, cw, 2 * cw).astype(bf16)
        cv[:, at] = (through(text, k + p, 2 * cw, 3 * cw) + biases[10:11, at]).astype(bf16)
        cq[:, at] = (through(c1, k + p, 0, cw) + biases[9:10, at]).astype(bf16)
        used(k + p)
    advance(2)
    for h in range(width // HEAD_DIM):
        at = slice(h * HEAD_DIM, (h + 1) * HEAD_DIM)
        probs = cross_probs(scale, cq[:, at], ck[:, at])
        oc[:, at] = dot(probs.astype(bf16), cv[:, at]).astype(bf16)
        if h % max(1, width // HEAD_DIM // 4) == 0:
            advance(1)
    advance(2)
    k += grid.np
    for p in range(grid.np):
        at = slice(p * cw, (p + 1) * cw)
        load(k + p).wait()
        x2[:, at] = x2[:, at] + through(oc, k + p, 3 * cw, 4 * cw) + biases[11:12, at]
        used(k + p)
    normed, _ = norm_parts(x2[...])
    a2[...] = (normed * (1.0 + vector(4)) + vector(3)).astype(bf16)
    advance(len(rest))
    for flow in flows[2:]:
        flow.finish()
    site.copies.finish()


def attention(grid, scale, owns, table, time, lat, text):
    rows, cols = owns[0].shape
    tokens, width = lat.shape
    sources = grid.ns
    heads = width // HEAD_DIM // sources
    length = sources * tokens
    blocks = jax.ShapeDtypeStruct((sources, heads, 3, HEAD_DIM, tokens), bf16)
    low = jax.ShapeDtypeStruct((tokens, width), bf16)
    high = jax.ShapeDtypeStruct((tokens, width), f32)
    word = jax.ShapeDtypeStruct(text.shape, bf16)
    return move(
        grid,
        lambda g, *refs: attention_kernel(g, scale, *refs),
        "attention",
        4 * gather_slots(grid) + 2 * grid.ns * heads + grid.ns,
        5 + 2 * heads,
        1,
        [gather_shape(grid, rows, cols)] * 4
        + [
            jax.ShapeDtypeStruct((sources, heads, HEAD_DIM, tokens), bf16),
            blocks,
            jax.ShapeDtypeStruct((heads, sources, HEAD_DIM, tokens), f32),
            jax.ShapeDtypeStruct((heads, sources, 8, tokens), f32),
            jax.ShapeDtypeStruct((tokens, width), bf16),
            jax.ShapeDtypeStruct((table.shape[0], width), f32),
            high,
            high,
            low,
            low,
            word,
            word,
            low,
            low,
        ],
        [HBM] * 4 + [VMEM] * 14,
        [HBM] * 4 + [VMEM] * 4,
        [pltpu.VMEM((sources, heads, HEAD_DIM, tokens), bf16)]
        + attend_scratch(blocks)
        + [
            pltpu.VMEM((grid.ns,) + table.shape, bf16),
            pltpu.VMEM(blocks.shape, bf16),
            pltpu.VMEM((2, grid.nz, grid.nc, rows, cols), bf16),
            pltpu.VMEM((tokens, width), bf16),
            pltpu.SemaphoreType.DMA((2,)),
        ],
        owns + (table, time, lat, text),
        56,
        pl.CostEstimate(
            flops=4 * heads * length * length * HEAD_DIM,
            bytes_accessed=60 * MIB,
            transcendentals=heads * length * length,
        ),
    )


def attention_back_kernel(
    grid,
    scale,
    grad_a,
    grad_b,
    in_ref,
    text_ref,
    qkv,
    wide,
    logs,
    own_ref,
    column_ref,
    back_ref,
    words_ref,
    *refs,
):
    scratch_a, scratch_b = refs[:5], refs[5:9]
    refs = refs[9:]
    text_got, text_low, grad_in, grad_qkv, keys, key_rows, values, grad_k, grad_v = refs[:9]
    site = Site(grid, *refs[9:])
    heads, sources = qkv.shape[1], qkv.shape[0]
    incoming = [ExchangeFlow(site, in_ref, grad_in, h) for h in range(heads)]
    text = ExchangeFlow(site, text_ref, text_got)
    queries = [ExchangeFlow(site, grad_qkv, back_ref, h, 0) for h in range(heads)]
    outgoing = [ExchangeFlow(site, grad_qkv, back_ref, h, pl.ds(1, 2)) for h in range(heads)]
    mine = scratch_a[0]
    a = ScatterFlow(site, grad_a, own_ref.at[0], *scratch_a)
    b = ScatterFlow(site, grad_b, None, mine, *scratch_b, column_ref=column_ref)
    blocks = a.blocks() + b.blocks()
    incoming[0].start()
    load_in_turn(blocks)
    steps = sequence(blocks)

    def due(kind, n):
        return 11.5 * n + {"F": 4, "S": 14, "T": 22}[kind]

    cut = max(i for i, (kind, n, _) in enumerate(steps) if due(kind, n) <= 10) + 1
    run(steps[:cut])
    incoming[0].finish()
    for flow in incoming[1:]:
        flow.start()
    text.start()
    times = [14 + 4.6 * i for i in range(heads * sources)]
    inside, rest = planned(steps[cut:], times, due)
    words = SpreadFlow(site, text_low, words_ref)

    def sum_text():
        text.finish()
        total = text_got[0].astype(f32)
        for n in range(1, grid.ns):
            total = total + text_got[n].astype(f32)
        text_low[...] = total.astype(bf16)
        words.start()

    inside.append((sources - 1, sum_text))

    def turn_of(i, carry):
        head, block = i // sources, turn(site.s, i, sources)
        for h in range(1, heads):
            pl.when(i == h * sources)(incoming[h].finish)

        @pl.when(i % sources == 0)
        def _():
            attend_back_head(qkv, head, keys, key_rows, values, grad_k, grad_v)

        attend_back_block(
            scale, qkv, grad_in, wide, logs, head, block, grad_qkv, keys, key_rows, values, grad_k, grad_v
        )

        @pl.when(i % sources == sources - 1)
        def _():
            attend_back_end(scale, head, grad_qkv, grad_k, grad_v)

        for h in range(heads):
            for r in range(sources):
                pl.when(i == h * sources + r)(functools.partial(queries[h].start_one, r))
            pl.when(i == (h + 1) * sources - 1)(outgoing[h].start)
        for at in sorted({n for n, _ in inside}):

            @pl.when(i == at)
            def _():
                for n, step in inside:
                    if n == at:
                        step()

        return carry

    lax.fori_loop(0, heads * sources, turn_of, 0)
    run(rest)
    for flow in [a, b, words] + queries + outgoing:
        flow.finish()
    site.copies.finish()


def attention_back(grid, scale, grads, blocks, text, qkv, wide, logs, rows, cols):
    shape = (grid.ay, grid.ax, grid.nz, grid.nc, rows, cols)
    sources, heads, _, dim, tokens = qkv.shape
    length = sources * tokens
    return move(
        grid,
        lambda g, *refs: attention_back_kernel(g, scale, *refs),
        "attention_back",
        2 * scatter_slots(grid) + grid.ns * (2 + 3 * heads),
        2 * grid.nz + 2 + 3 * heads,
        2,
        [
            jax.ShapeDtypeStruct((1, rows, cols), f32),
            jax.ShapeDtypeStruct((grid.nz, rows, cols), bf16),
            jax.ShapeDtypeStruct(qkv.shape, bf16),
            jax.ShapeDtypeStruct(text.shape, bf16),
        ],
        [VMEM, VMEM, HBM, HBM],
        [HBM] * 4 + [VMEM] * 3,
        scatter_scratch(grid, rows, cols)
        + scatter_scratch(grid, rows, cols, mine=False)
        + [
            pltpu.VMEM(text.shape, bf16),
            pltpu.VMEM(text.shape[1:], bf16),
            pltpu.VMEM((sources, heads, dim, tokens), bf16),
            pltpu.VMEM(qkv.shape, bf16),
        ]
        + attend_back_scratch(qkv),
        tuple(g.reshape(shape) for g in grads) + (blocks, text, qkv, wide, logs),
        60,
        pl.CostEstimate(
            flops=10 * heads * length * length * dim,
            bytes_accessed=60 * MIB,
            transcendentals=heads * length * length,
        ),
    )


def dot(left, right, kind="nn"):
    contract = ((0 if kind[0] == "t" else 1,), (1 if kind[1] == "t" else 0,))
    return lax.dot_general(left, right, (contract, ((), ())), preferred_element_type=f32)


def norm_parts(tokens_in):
    center = tokens_in - jnp.mean(tokens_in, axis=-1, keepdims=True)
    spread = jnp.mean(center * center, axis=-1, keepdims=True)
    rate = lax.rsqrt(spread + norm_eps)
    return center * rate, rate


def norm_back(grad, normed, rate, gain):
    inner = grad * gain
    mean = jnp.mean(inner, axis=-1, keepdims=True)
    along = jnp.mean(inner * normed, axis=-1, keepdims=True)
    return rate * (inner - mean - normed * along)


def column(rows_ref, n):
    return rows_ref[n : n + 1, :]


def cross_probs(scale, query, keys):
    scores = dot(query, keys, "nt") * scale
    part = jnp.exp(scores - jnp.max(scores, axis=-1, keepdims=True))
    return part / jnp.sum(part, axis=-1, keepdims=True)


def gelu_pair(pre):
    rate = math.sqrt(2.0 / math.pi)
    square = pre * pre
    bend = jnp.tanh(rate * pre * (1.0 + 0.044715 * square))
    half = 0.5 * (1.0 + bend)
    slope = half + 0.5 * pre * (1.0 - bend * bend) * rate * (1.0 + 3 * 0.044715 * square)
    return pre * half, slope


def mlp_kernel(
    a2, cot, x2, up, down, b1, rows_ref, out, da2, grad_up, grad_down, du_sum, sums, a2_t, dz3, dz3_t, z3
):
    p = pl.program_id(0)

    @pl.when(p == 0)
    def _():
        back = (column(rows_ref, 0) * cot[...].astype(f32)).astype(bf16)
        dz3[...] = back
        dz3_t[...] = flip(back).astype(bf16)
        a2_t[...] = flip(a2[...]).astype(bf16)
        sums[0:1, :] = jnp.sum(back.astype(f32), axis=0, keepdims=True)

    pre = dot(a2[...], up[0]) + b1[0]
    act, slope = gelu_pair(pre)
    hidden = act.astype(bf16)
    grad = (dot(dz3[...], down[0]) * slope).astype(bf16)
    du_sum[0] = jnp.sum(grad.astype(f32), axis=0, keepdims=True)
    part = dot(hidden, down[0], "nt")
    back = dot(grad, up[0], "nt")

    @pl.when(p == 0)
    def _():
        z3[...] = part
        da2[...] = back

    @pl.when(p > 0)
    def _():
        z3[...] += part
        da2[...] += back

    grad_up[0] = dot(a2_t[...], grad).astype(bf16)
    grad_down[0] = dot(dz3_t[...], hidden).astype(bf16)

    @pl.when(p == pl.num_programs(0) - 1)
    def _():
        branch = z3[...] + column(rows_ref, 1)
        out[...] = (x2[...] + column(rows_ref, 0) * branch).astype(bf16)
        sums[1:2, :] = jnp.sum(cot[...].astype(f32) * branch, axis=0, keepdims=True)


def mlp(a2, cot, x2, up, down, b1, rows):
    tokens, width = a2.shape
    np_, _, cols = up.shape
    block = pl.BlockSpec((1, width, cols), lambda p: (p, 0, 0))
    row = pl.BlockSpec((1, 1, cols), lambda p: (p, 0, 0))
    return pl.pallas_call(
        mlp_kernel,
        name="mlp",
        grid=(np_,),
        out_shape=[
            jax.ShapeDtypeStruct((tokens, width), bf16),
            jax.ShapeDtypeStruct((tokens, width), f32),
            jax.ShapeDtypeStruct(up.shape, bf16),
            jax.ShapeDtypeStruct(down.shape, bf16),
            jax.ShapeDtypeStruct((np_, 1, cols), f32),
            jax.ShapeDtypeStruct((8, width), f32),
        ],
        in_specs=[VMEM, VMEM, VMEM, block, block, row, VMEM],
        out_specs=[VMEM, VMEM, block, block, row, VMEM],
        scratch_shapes=[
            pltpu.VMEM((width, tokens), bf16),
            pltpu.VMEM((tokens, width), bf16),
            pltpu.VMEM((width, tokens), bf16),
            pltpu.VMEM((tokens, width), f32),
        ],
        compiler_params=pltpu.CompilerParams(vmem_limit_bytes=56 * MIB),
        cost_estimate=pl.CostEstimate(
            flops=12 * tokens * width * cols * np_,
            bytes_accessed=44 * MIB,
            transcendentals=tokens * cols * np_,
        ),
    )(a2, cot, x2, up, down, b1, rows)


def cross_back_kernel(
    grid,
    scale,
    da2,
    x2,
    cot,
    z1,
    cq,
    ck,
    cv,
    c1,
    oc,
    text,
    rows_ref,
    w_self,
    w_cross,
    grad_ref,
    dx1,
    do_t,
    dz1,
    text_part,
    sums,
    own_ref,
    grad_cross,
    *refs,
):
    scratch, refs = refs[:5], refs[5:]
    doc, dz2, dcq, part_k, part_v, left, wo, wc, stage, sems = refs[:10]
    low = doc
    np_, width, wide = w_self.shape
    cw = wide // 4
    lo = 3 * cw // 128 * 128
    load_o = pltpu.make_async_copy(w_self.at[:, :, pl.ds(lo, wide - lo)], wo, sems.at[0])
    load_c = pltpu.make_async_copy(w_cross, wc, sems.at[1])
    load_c.start()
    load_o.start()
    site = Site(grid, *refs[10:])
    flow = ScatterFlow(site, grad_ref, own_ref.at[0], *scratch)
    load_in_turn(flow.blocks())
    steps = sequence(flow.blocks())

    def advance(count):
        run(steps[:count])
        del steps[:count]

    def total(n, matrix):
        sums[n : n + 1, :] = jnp.sum(matrix, axis=0, keepdims=True)

    normed, rate = norm_parts(x2[...])
    grad = da2[...]
    total(0, grad)
    total(1, grad * normed)
    grad = cot[...].astype(f32) + norm_back(grad, normed, rate, 1.0 + column(rows_ref, 0))
    dx1[...] = grad
    dz2[...] = grad.astype(bf16)
    total(2, dz2[...].astype(f32))
    advance(2)
    load_c.wait()

    def back(source, w, first):
        found = None
        for p in range(np_):
            part = dot(source[:, p * cw : (p + 1) * cw], w[p, :, first : first + cw], "nt")
            found = part if found is None else found + part
        return found

    doc[...] = back(dz2, wc, 3 * cw).astype(bf16)
    advance(1)
    half = width // HEAD_DIM // 2
    for h in range(width // HEAD_DIM):
        at = slice(h * HEAD_DIM, (h + 1) * HEAD_DIM)
        query, keys, grad_h = cq[:, at], ck[:, at], doc[:, at]
        probs = cross_probs(scale, query, keys)
        grad_p = dot(grad_h, cv[:, at], "nt")
        inner = jnp.sum(grad_p * probs, axis=-1, keepdims=True)
        grad_s = (probs * (grad_p - inner)).astype(bf16)
        dcq[:, at] = (dot(grad_s, keys) * scale).astype(bf16)
        part_k[:, at] = (dot(grad_s, query, "tn") * scale).astype(bf16)
        whole = dot(probs.astype(bf16), grad_h, "tn")
        part_v[:, at] = whole.astype(bf16)
        sums[4:5, at] = jnp.sum(whole, axis=0, keepdims=True)
        if h == half:
            advance(2)
    total(3, dcq[...].astype(f32))
    advance(2)
    grad = dx1[...] + back(dcq, wc, 0)
    dx1[...] = grad
    total(5, grad * z1[...])
    low[...] = (column(rows_ref, 1) * grad).astype(bf16)
    total(6, low[...].astype(f32))
    for p in range(np_):
        dz1[p] = low[:, p * cw : (p + 1) * cw]
    load_o.wait()
    do_t[...] = jnp.transpose(back(low, wo, 3 * cw - lo)).astype(bf16)
    advance(1)
    words = ck.shape[0]
    text_part[...] = jnp.zeros_like(text_part)
    text_part[0:words, 0:width] = part_k[...]
    text_part[0:words, width : 2 * width] = part_v[...]
    left[0] = flip(c1[...]).astype(bf16)
    left[1] = flip(oc[...]).astype(bf16)
    words_t = flip(text[...]).astype(bf16)

    def store(p):
        return pltpu.make_async_copy(stage.at[p % 2], grad_cross.at[p], sems.at[2 + p % 2])

    for p in range(np_):
        at = slice(p * cw, (p + 1) * cw)
        if p >= 2:
            store(p - 2).wait()
        into = stage.at[p % 2]
        into[:, 0:cw] = dot(left[0], dcq[:, at]).astype(bf16)
        into[:, cw : 2 * cw] = dot(words_t, part_k[:, at]).astype(bf16)
        into[:, 2 * cw : 3 * cw] = dot(words_t, part_v[:, at]).astype(bf16)
        into[:, 3 * cw : 4 * cw] = dot(left[1], dz2[:, at]).astype(bf16)
        store(p).start()
        if p % (np_ // 4 if np_ >= 4 else 1) == 0:
            advance(1)
    advance(len(steps))
    for p in range(max(0, np_ - 2), np_):
        store(p).wait()
    flow.finish()
    site.copies.finish()


def cross_backward(grid, scale, da2, x2, cot, z1, cq, ck, cv, c1, oc, text, rows, w_self, w_cross, grad, rows_padded, own_rows):
    tokens, width = x2.shape
    np_, _, wide = w_self.shape
    words = ck.shape[0]
    lo = 3 * (wide // 4) // 128 * 128
    low = pltpu.VMEM((tokens, width), bf16)
    word = pltpu.VMEM((words, width), bf16)
    return move(
        grid,
        lambda g, *refs: cross_back_kernel(g, scale, *refs),
        "cross_backward",
        scatter_slots(grid),
        grid.nz,
        5,
        [
            jax.ShapeDtypeStruct((tokens, width), f32),
            jax.ShapeDtypeStruct((width, tokens), bf16),
            jax.ShapeDtypeStruct((np_, tokens, wide // 4), bf16),
            jax.ShapeDtypeStruct((rows_padded, 2 * width), bf16),
            jax.ShapeDtypeStruct((8, width), f32),
            jax.ShapeDtypeStruct((1, own_rows, wide), f32),
            jax.ShapeDtypeStruct(w_cross.shape, bf16),
        ],
        [VMEM] * 6 + [HBM],
        [VMEM] * 11 + [HBM] * 3,
        scatter_scratch(grid, own_rows, wide)
        + [
            low,
            low,
            low,
            word,
            word,
            pltpu.VMEM((2, width, tokens), bf16),
            pltpu.VMEM((np_, width, wide - lo), bf16),
            pltpu.VMEM(w_cross.shape, bf16),
            pltpu.VMEM((2, width, wide), bf16),
            pltpu.SemaphoreType.DMA((4,)),
        ],
        (
            da2,
            x2,
            cot,
            z1,
            cq,
            ck,
            cv,
            c1,
            oc,
            text,
            rows,
            w_self,
            w_cross,
            grad.reshape(grid.ay, grid.ax, grid.nz, grid.nc, own_rows, wide),
        ),
        63,
        pl.CostEstimate(
            flops=11 * tokens * width * width, bytes_accessed=50 * MIB, transcendentals=0
        ),
    )


def last_kernel(
    grid,
    a1,
    grad_qkv,
    att_t,
    dz1,
    lat,
    dx1,
    words,
    rows_ref,
    sums,
    mlp_sums,
    du_sums,
    own_up,
    own_down,
    w_self,
    w_cross,
    column_ref,
    own_ref,
    tokens_ref,
    words_ref,
    time_ref,
    own_table,
    norm_ref,
    *refs,
):
    scratch, refs = refs[:4], refs[4:]
    slab, a1_t, by_dp, back_t, weights, table_all, table_in = refs[:7]
    column_own, column_got = refs[7:9]
    table_got, table_sum, table_dp, tile, tile_got, tile_sum, tile_dp, sems = refs[9:17]
    np_, width, wide = w_self.shape
    tokens = a1.shape[0]
    cw = wide // 4
    nc, rows = grid.nc, wide and slab.shape[4]
    lo, hi = cw // 128 * 128, min(wide, -(-3 * cw // 128) * 128)
    loads = [
        pltpu.make_async_copy(w_self.at[p], weights.at[p % 2], sems.at[p % 2]) for p in range(np_)
    ] + [
        pltpu.make_async_copy(
            w_cross.at[p, :, pl.ds(lo, hi - lo)],
            weights.at[(np_ + p) % 2, :, pl.ds(0, hi - lo)],
            sems.at[(np_ + p) % 2],
        )
        for p in range(np_)
    ]
    loads[0].start()
    loads[1].start()

    def weight(k):
        loads[k].wait()
        return weights.at[k % 2]

    def used(k):
        if k + 2 < len(loads):
            loads[k + 2].start()

    site = Site(grid, *refs[17:])
    flow = NearScatterFlow(site, slab, own_ref.at[0], None, *scratch)
    column_sum = ColumnSum(site, column_ref, own_ref.at[1], column_own, column_got)
    column_sum.start()
    flat = flip(a1[...]).astype(bf16)
    span = nc * rows
    for z in range(grid.nz):
        a1_t[z] = flat[z * span : (z + 1) * span]
    heads = grad_qkv.shape[1]
    per_block = cw // HEAD_DIM
    for p in range(np_):
        for h in range(per_block):
            source, head = divmod(p * per_block + h, heads)
            for j in range(3):
                at = j * cw + h * HEAD_DIM
                by_dp[p, at : at + HEAD_DIM] = grad_qkv[source, head, j]

    for n in range(grid.nz):
        zone = flow.zone(n)
        for p in range(np_):
            part = dot(a1_t[zone], by_dp[p], "nt").astype(bf16)
            rest = dot(att_t[zone], dz1[p]).astype(bf16)
            for c in range(nc):
                at = slice(c * rows, (c + 1) * rows)
                slab[n, c, p // grid.ax, p % grid.ax, :, 0 : 3 * cw] = part[at]
                slab[n, c, p // grid.ax, p % grid.ax, :, 3 * cw :] = rest[at]
        flow.load(n)
        if n == 1:
            flow.first(0)
    steps = sequence(flow.blocks())[1:]

    def advance(count):
        run(steps[:count])
        del steps[:count]

    advance(2)
    for p in range(np_):
        part = dot(weight(p)[:, 0 : 3 * cw], by_dp[p])
        back_t[...] = part if p == 0 else back_t[...] + part
        used(p)
        if np_ < 8 or p % 4 == 0:
            advance(1)
    grad = jnp.transpose(back_t[...])
    normed, rate = norm_parts(lat[...].astype(f32))
    tokens_ref[...] = dx1[...] + norm_back(grad, normed, rate, 1.0 + column(rows_ref, 0))
    for at, source, n in (
        (2, sums, 5),
        (3, sums, 0),
        (4, sums, 1),
        (5, mlp_sums, 1),
        (8, sums, 6),
        (9, sums, 3),
        (10, sums, 4),
        (11, sums, 2),
        (12, mlp_sums, 0),
    ):
        table_all[at : at + 1, :] = source[n : n + 1, :]
    for p in range(np_):
        at, lane = 13 + p * wide // width, p * wide % width
        table_all[at : at + 1, lane : lane + wide] = du_sums[p]
    table_all[0:1, :] = jnp.sum(grad, axis=0, keepdims=True)
    table_all[1:2, :] = jnp.sum(grad * normed, axis=0, keepdims=True)
    ones = jnp.ones((8, tokens), bf16)
    for p in range(np_):
        whole = dot(ones, by_dp[p], "nt")
        at = slice(p * cw, (p + 1) * cw)
        table_all[6:7, at] = whole[0:1, 0:cw]
        table_all[7:8, at] = whole[0:1, 2 * cw : 3 * cw]
    part = width // grid.ns
    for n in range(grid.ns):
        table_in[n] = table_all[0 : table_in.shape[1], n * part : (n + 1) * part]
    table = ExchangeFlow(site, table_in, table_got)
    table.start()
    advance(2)
    found = None
    for p in range(np_):
        w = weight(np_ + p)
        at = slice(p * cw, (p + 1) * cw)
        both = dot(words[:, at], w[:, cw - lo : 2 * cw - lo], "nt")
        at = slice(width + p * cw, width + (p + 1) * cw)
        both = both + dot(words[:, at], w[:, 2 * cw - lo : 3 * cw - lo], "nt")
        found = both if found is None else found + both
        used(np_ + p)
    words_ref[...] = found[0 : words_ref.shape[0]]
    table.finish()
    total = table_got[0]
    for n in range(1, grid.ns):
        total = total + table_got[n]
    table_sum[...] = total
    whole = SpreadFlow(site, table_sum, time_ref)
    whole.start()
    over = SpreadFlow(site, table_sum, table_dp, over_dp=True)
    over.start()
    advance(max(0, len(steps) - 2))
    over.finish()
    total = table_dp[0]
    for n in range(1, grid.np):
        total = total + table_dp[n]
    own_table[...] = total
    column_sum.finish()
    square = jnp.sum(own_ref[1] * own_ref[1], keepdims=True)
    for done in (own_up, own_down):
        square = square + jnp.sum(done[0] * done[0], keepdims=True)
    square = square + jnp.where(site.p == 0, 1.0, 0.0) * jnp.sum(total * total, keepdims=True)
    advance(2)
    flow.finish()
    square = square + jnp.sum(own_ref[0] * own_ref[0], keepdims=True)
    tile[...] = jnp.broadcast_to(square, tile.shape)
    near = SpreadFlow(site, tile, tile_got)
    near.start()
    near.finish()
    total = tile_got[0]
    for n in range(1, grid.ns):
        total = total + tile_got[n]
    tile_sum[...] = total
    far = SpreadFlow(site, tile_sum, tile_dp, over_dp=True)
    far.start()
    far.finish()
    total = tile_dp[0]
    for n in range(1, grid.np):
        total = total + tile_dp[n]
    norm_ref[...] = total
    whole.finish()
    site.copies.finish()


def last_sums(grid, a1, grad_qkv, att_t, dz1, lat, dx1, words, text_count, rows_in, sums, owns, w_self, w_cross, column, table_rows):
    np_, width, wide = w_self.shape
    rows, cols = column.shape[1:]
    tokens = a1.shape[0]
    small = (table_rows, width // grid.ns)
    tile = (8, 128)
    return move(
        grid,
        last_kernel,
        "last_sums",
        scatter_slots(grid) + grid.nz + 3 * grid.ns + 2 * grid.np,
        6,
        3,
        [
            jax.ShapeDtypeStruct((2, rows, cols), f32),
            jax.ShapeDtypeStruct((tokens, width), f32),
            jax.ShapeDtypeStruct((text_count, width), f32),
            jax.ShapeDtypeStruct((grid.ns,) + small, f32),
            jax.ShapeDtypeStruct(small, f32),
            jax.ShapeDtypeStruct(tile, f32),
        ],
        [VMEM, VMEM, VMEM, HBM, VMEM, VMEM],
        [VMEM] * 13 + [HBM] * 3,
        scatter_scratch(grid, rows, cols, mine=False)
        + [
            pltpu.VMEM((grid.nz, grid.nc, grid.ay, grid.ax, rows, cols), bf16),
            pltpu.VMEM((grid.nz, grid.nc * rows, tokens), bf16),
            pltpu.VMEM((np_, 3 * (wide // 4), tokens), bf16),
            pltpu.VMEM((width, tokens), f32),
            pltpu.VMEM((2, width, wide), bf16),
            pltpu.VMEM((-(-table_rows // 8) * 8, width), f32),
            pltpu.VMEM((grid.ns,) + small, f32),
            pltpu.VMEM((rows, cols), bf16),
            pltpu.VMEM((max(1, grid.nz - 1), rows, cols), bf16),
            pltpu.VMEM((grid.ns,) + small, f32),
            pltpu.VMEM(small, f32),
            pltpu.VMEM((grid.np,) + small, f32),
            pltpu.VMEM(tile, f32),
            pltpu.VMEM((grid.ns,) + tile, f32),
            pltpu.VMEM(tile, f32),
            pltpu.VMEM((grid.np,) + tile, f32),
            pltpu.SemaphoreType.DMA((2,)),
        ],
        (
            a1,
            grad_qkv,
            att_t.reshape(grid.nz, grid.nc * rows, tokens),
            dz1,
            lat,
            dx1,
            words,
            rows_in,
            *sums,
            *owns,
            w_self,
            w_cross,
            column,
        ),
        60,
    )


def adam_kernel(
    norm, grad_attn, grad_up, grad_down, w_attn, f_attn, s_attn, w_mlp, f_mlp, s_mlp, *outs
):
    factor = jnp.minimum(1.0, clip_norm / (norm[0:1, 0:1] + 1e-06))
    width = w_attn.shape[2]
    for j in range(w_attn.shape[0]):
        grad = grad_attn[0, :, j * width : (j + 1) * width]
        new, first, second = adam_step(w_attn[j], grad, f_attn[j], s_attn[j], factor)
        outs[0][j], outs[1][j], outs[2][j], outs[3][j] = new, new.astype(bf16), first, second
    grad = jnp.where(pl.program_id(0) == 0, grad_up[0], grad_down[0])
    new, first, second = adam_step(w_mlp[0], grad, f_mlp[0], s_mlp[0], factor)
    outs[4][0], outs[5][0], outs[6][0], outs[7][0] = new, new.astype(bf16), first, second


def adam(norm, grad_attn, grad_up, grad_down, attn, mlp_state):
    rows, cols = grad_up.shape[1:]
    width = attn[0].shape[2]
    part = rows // 3 if rows % 48 == 0 else rows
    slab = pl.BlockSpec((1, part, cols), lambda k, r: (k, r, 0))
    one = pl.BlockSpec((1, part, cols), lambda k, r: (0, r, 0))
    four = pl.BlockSpec((4, part, width), lambda k, r: (k, r, 0))

    def shapes(array):
        full = jax.ShapeDtypeStruct(array.shape, f32)
        return [full, jax.ShapeDtypeStruct(array.shape, bf16), full, full]

    return pl.pallas_call(
        adam_kernel,
        name="adam",
        grid=(2, rows // part),
        out_shape=shapes(attn[0]) + shapes(mlp_state[0]),
        in_specs=[VMEM, slab, one, one] + [four] * 3 + [slab] * 3,
        out_specs=[four] * 4 + [slab] * 4,
        compiler_params=pltpu.CompilerParams(vmem_limit_bytes=40 * MIB),
        cost_estimate=pl.CostEstimate(
            flops=40 * attn[0].size, bytes_accessed=24 * MIB, transcendentals=2 * attn[0].size
        ),
    )(norm, grad_attn, grad_up, grad_down, *attn, *mlp_state)


def layer_norm(tokens_in):
    center = tokens_in - jnp.mean(tokens_in, axis=-1, keepdims=True)
    spread = jnp.mean(center * center, axis=-1, keepdims=True)
    return center * lax.rsqrt(spread + norm_eps)


def modulate(tokens_in, shift_row, scale_row):
    return layer_norm(tokens_in) * (1.0 + scale_row) + shift_row


def adam_step(weight, gradient, first_moment, second_moment, factor):
    clipped = gradient * factor
    first_new = first_decay * first_moment + (1.0 - first_decay) * clipped
    second_new = second_decay * second_moment + (1.0 - second_decay) * clipped * clipped
    first_hat = first_new / (1.0 - first_decay**STEP)
    second_hat = second_new / (1.0 - second_decay**STEP)
    updated = weight - learn_rate * (
        first_hat / (jnp.sqrt(second_hat) + adam_eps) + weight_decay * weight
    )
    return (updated, first_new, second_new)


def body(
    grid,
    latents,
    time_embed,
    text_tokens,
    cotangent,
    w_attn,
    w_mlp,
    bias_table,
    attn_first,
    attn_second,
    mlp_first,
    mlp_second,
    table_first,
    table_second,
):
    np_, ns = grid.np, grid.ns
    tokens_in = latents[0].astype(f32)
    rows, width = tokens_in.shape
    text_rows = text_tokens[0]
    text_count = text_rows.shape[0]
    heads = width // HEAD_DIM
    per_block = heads // np_
    local_heads = heads // ns
    scale = HEAD_DIM ** (-0.5)
    own_rows, own_cols = w_attn.shape[1], w_attn.shape[2]
    wide = 4 * own_cols

    def pack(matrices):
        return matrices.reshape(2, 4, own_rows, own_cols).transpose(0, 2, 1, 3).reshape(2, own_rows, wide)

    attn_low = pack(w_attn.astype(bf16))
    mlp_low = w_mlp.astype(bf16)
    own = (attn_low[0], attn_low[1], mlp_low[0], mlp_low[1])
    forward = attention(
        grid, scale, own, bias_table.astype(bf16), time_embed[0], latents[0], text_rows
    )
    w_self, w_cross, w_up, w_down = [w.reshape(np_, width, wide) for w in forward[:4]]
    attended_t, qkv, mixed_wide, logs, act_in, biases = forward[4:10]
    z1, x2, c1, cq, text_k, text_v, cross_out, a2 = forward[10:]
    modulation = biases[0:6] + time_embed[0].astype(f32)
    attended_t = attended_t.reshape(width, rows)

    block_out, da2, grad_up, grad_down, du_sums, mlp_sums = mlp(
        a2,
        cotangent[0],
        x2,
        w_up,
        w_down,
        biases[13:17].reshape(np_, 1, wide),
        jnp.stack([modulation[5], biases[12]]),
    )
    text_share = -(-text_count // (8 * ns)) * 8
    grad_first, grad_attended, dz1, text_part, sums, own_up, grad_cross = cross_backward(
        grid,
        scale,
        da2,
        x2,
        cotangent[0],
        z1,
        cq,
        text_k,
        text_v,
        c1,
        cross_out,
        text_rows,
        jnp.stack([modulation[4], modulation[2]]),
        w_self,
        w_cross,
        grad_up,
        ns * text_share,
        own_rows,
    )
    own_down, grad_column, grad_qkv, text_sum = attention_back(
        grid,
        scale,
        (grad_down, grad_cross),
        grad_attended.reshape(ns, local_heads, HEAD_DIM, rows),
        text_part.reshape(ns, text_share, 2 * width),
        qkv,
        mixed_wide,
        logs,
        own_rows,
        wide,
    )
    table_rows = bias_table.shape[0]
    own_attn, grad_tokens, grad_words, time_table, own_table, squares = last_sums(
        grid,
        act_in,
        grad_qkv,
        attended_t,
        dz1,
        latents[0],
        grad_first,
        text_sum.reshape(ns * text_share, 2 * width),
        text_count,
        modulation[1:2],
        (sums, mlp_sums, du_sums),
        (own_up, own_down),
        w_self,
        w_cross,
        grad_column,
        table_rows,
    )
    grad_time = time_table[:, :6].transpose(1, 0, 2).reshape(6, width)
    norms = jnp.sqrt(squares)
    grad_norm = norms[0, 0]
    factor = jnp.minimum(1.0, clip_norm / (grad_norm + 1e-06))
    (
        attn_new,
        attn_copy,
        attn_first_new,
        attn_second_new,
        mlp_new,
        mlp_copy,
        mlp_first_new,
        mlp_second_new,
    ) = adam(
        norms,
        own_attn,
        own_up,
        own_down,
        (w_attn, attn_first, attn_second),
        (w_mlp, mlp_first, mlp_second),
    )
    table_new, table_first_new, table_second_new = adam_step(
        bias_table, own_table, table_first, table_second, factor
    )
    return (
        block_out[None],
        grad_tokens[None],
        grad_time[None],
        grad_words[None],
        grad_norm,
        attn_new,
        attn_copy,
        attn_first_new,
        attn_second_new,
        mlp_new,
        mlp_copy,
        mlp_first_new,
        mlp_second_new,
        table_new,
        table_new.astype(bf16),
        table_first_new,
        table_second_new,
        own_table[12],
    )


def solution(mesh):
    return jax.shard_map(
        functools.partial(body, Grid(mesh)),
        mesh=mesh,
        in_specs=(
            P("dp", "seq", None),
            P("dp", None, None),
            P("dp", None, None),
            P("dp", "seq", None),
            P(None, "seq", "dp"),
            P(None, "seq", "dp"),
            P(None, "seq"),
            P(None, "seq", "dp"),
            P(None, "seq", "dp"),
            P(None, "seq", "dp"),
            P(None, "seq", "dp"),
            P(None, "seq"),
            P(None, "seq"),
        ),
        out_specs=(
            P("dp", "seq", None),
            P("dp", "seq", None),
            P("dp", None, None),
            P("dp", None, None),
            P(),
            P(None, "seq", "dp"),
            P(None, "seq", "dp"),
            P(None, "seq", "dp"),
            P(None, "seq", "dp"),
            P(None, "seq", "dp"),
            P(None, "seq", "dp"),
            P(None, "seq", "dp"),
            P(None, "seq", "dp"),
            P(None, "seq"),
            P(None, "seq"),
            P(None, "seq"),
            P(None, "seq"),
            P("seq"),
        ),
        check_vma=False,
    )
```
